256 devices in a mesh: pipe: 2 (over z_lo), rep: 4 (over z_hi), shard: 32 (over y, x, core).
Axes of the slice: x: 4, y: 4, z: 8 (z_hi: 4, z_lo: 2; z = z_hi * 2 + z_lo), core: 2. Of those that a mesh axis runs over, the one named last changes fastest.
Arguments:
- hidden_in: bfloat16 [2, 16384, 8192], P('pipe', ('rep', 'shard')), may hold values from -600 to 600
- query_rows: bfloat16 [2, 16384, 4096], P('pipe', ('rep', 'shard')), may hold values from -160 to 160
- key_rows: bfloat16 [2, 16384, 512], P('pipe', ('rep', 'shard')), may hold values from -6 to 6
- context_grad: bfloat16 [2, 16384, 4096], P('pipe', ('rep', 'shard')), may hold values from -6 to 6
- stream_top: bfloat16 [16384, 8192], P(('rep', 'shard')), may hold values from -4 to 4
- norm_gain: float32 [2, 8192], P('pipe'), may hold values from 0.1 to 1.9
- value_weight: bfloat16 [2, 8192, 512], P('pipe', 'shard'), may hold values from -0.0625 to 0.0625
Outputs:
- stream_grad: bfloat16 [2, 16384, 8192], P('pipe', ('rep', 'shard'))
- query_grad: bfloat16 [2, 16384, 4096], P('pipe', ('rep', 'shard'))
- key_grad: bfloat16 [2, 16384, 512], P('pipe', ('rep', 'shard'))
- value_weight_grad: float32 [2, 8192, 512], P('pipe', 'shard')
- gain_grad: float32 [2, 8192], P('pipe', 'shard')
The draws below stay inside these ranges and needn't reach their ends.
All inputs are finite; a program needn't handle non-finite values.
Results may differ from the reference program's by a relative error of at most 0.025.
Values may be sent and summed in bfloat16 or wider, within the bound.
A program may use at most 128 MiB of HBM per device.

```python
import jax
import jax.numpy as jnp
from jax import lax

D = 8192
HEAD_DIM = 128
QHEADS = 32
KVHEADS = 4
TOK_DEV = 128
SECTIONS = 2
QW = 4096
KVW = 512
TOKENS = 16384


def shared_draws(key):
    key_query, key_key = jax.random.split(key, 2)
    query_raw = jax.random.normal(key_query, (SECTIONS, TOKENS, QHEADS * HEAD_DIM), jnp.float32)
    key_raw = jax.random.normal(key_key, (SECTIONS, TOKENS, KVHEADS * HEAD_DIM), jnp.float32)
    return (query_raw, key_raw)


def draw_query_rows(key, part):
    query_raw, key_raw = shared_draws(key)
    result = jnp.clip(query_raw, -6.0, 6.0)
    return result.astype(jnp.bfloat16)


def draw_key_rows(key, part):
    query_raw, key_raw = shared_draws(key)
    result = jnp.clip(key_raw, -6.0, 6.0)
    return result.astype(jnp.bfloat16)


def draw_hidden_in(key, part):
    key = jax.random.fold_in(key, 11)
    key_base, key_row, key_column = jax.random.split(key, 3)
    full_shape = (SECTIONS, TOKENS, D)
    row_scale = jnp.exp(jax.random.uniform(key_row, (SECTIONS, TOKENS, 1), jnp.float32, 0.0, 2.3))
    noise_base = jnp.clip(jax.random.normal(key_base, full_shape, jnp.float32), -4.0, 4.0)
    column_scale = jnp.exp(jax.random.uniform(key_column, (SECTIONS, 1, D), jnp.float32, 0.0, 2.3))
    result = jnp.clip(row_scale * (column_scale * noise_base), -600.0, 600.0)
    return result.astype(jnp.bfloat16)


def level_of(own_key, dims, cuts, low, high):
    gain = 1.0
    for dim, blocks in cuts:
        heights = jax.random.uniform(jax.random.fold_in(jax.random.fold_in(own_key, 6), dim), (blocks,), jnp.float32, low / len(cuts), high / len(cuts))
        gain = gain * jnp.repeat(jnp.exp(heights), dims[dim] // blocks).reshape((-1,) + (1,) * (len(dims) - 1 - dim))
    return gain


def gaussian(rng, dims, scale, reach, cuts=(), dtype=jnp.bfloat16):
    gain = level_of(rng, dims, cuts, -0.22, 0.18) if cuts else 1.0
    values = jax.random.normal(rng, dims, jnp.float32) * scale * gain
    return jnp.minimum(jnp.maximum(values, -reach), reach).astype(dtype)


def setup_inputs(seed: int = 0) -> dict:
    key_of = jax.random.split(jax.random.key(seed), 8)
    hidden_in = draw_hidden_in(jax.random.fold_in(key_of[7], 71), 0)
    query_rows = draw_query_rows(jax.random.fold_in(key_of[7], 71), 0)
    key_rows = draw_key_rows(jax.random.fold_in(key_of[7], 71), 0)
    context_grad = gaussian(key_of[3], (SECTIONS, TOKENS, QW), 1.0, 6.0, ((0, 2), (1, 128)))
    stream_top = gaussian(key_of[4], (TOKENS, D), 0.3, 4.0, ((0, 128),))
    norm_gain = jnp.clip(1.0 + 0.18 * jax.random.normal(key_of[5], (SECTIONS, D), jnp.float32), 0.1, 1.9)
    value_weight = gaussian(key_of[6], (SECTIONS, D, KVW), D ** -0.5, 0.0625, ((0, 2), (1, 32)))
    return {"hidden_in": hidden_in, "query_rows": query_rows, "key_rows": key_rows, "context_grad": context_grad, "stream_top": stream_top, "norm_gain": norm_gain, "value_weight": value_weight}


EPSILON = 1e-05

def attend_back(query_rows, key_rows, values, context_grad):
    row_count = query_rows.shape[0]
    groups = QHEADS // KVHEADS
    score_scale = 1.0 / HEAD_DIM ** 0.5
    query_heads = query_rows.astype(jnp.float32).reshape(row_count, KVHEADS, groups, HEAD_DIM)
    key_heads = key_rows.astype(jnp.float32).reshape(row_count, KVHEADS, HEAD_DIM)
    value_heads = values.astype(jnp.float32).reshape(row_count, KVHEADS, HEAD_DIM)
    grad_heads = context_grad.astype(jnp.float32).reshape(row_count, KVHEADS, groups, HEAD_DIM)
    scores = jnp.einsum('tkgd,ukd->kgtu', query_heads, key_heads) * score_scale
    positions = jnp.arange(row_count)
    allowed = positions[None, :] <= positions[:, None]
    scores = jnp.where(allowed, scores, -1e+30)
    top_score = lax.optimization_barrier(jnp.max(scores, axis=-1, keepdims=True))
    weights_raw = jnp.exp(scores - top_score)
    probs = weights_raw / lax.optimization_barrier(jnp.sum(weights_raw, axis=-1, keepdims=True))
    probs_low = probs.astype(jnp.bfloat16)
    grad_prob = jnp.einsum('tkgd,ukd->kgtu', grad_heads, value_heads)
    row_dot = lax.optimization_barrier(jnp.sum(probs * grad_prob, axis=-1, keepdims=True))
    grad_score = (probs * (grad_prob - row_dot) * score_scale).astype(jnp.bfloat16)
    grad_wide = grad_score.astype(jnp.float32)
    query_grad = jnp.einsum('kgtu,ukd->tkgd', grad_wide, key_heads)
    key_grad = jnp.einsum('kgtu,tkgd->ukd', grad_wide, query_heads)
    value_grad = jnp.einsum('kgtu,tkgd->ukd', probs_low.astype(jnp.float32), grad_heads)
    return (query_grad.reshape(row_count, QW).astype(jnp.bfloat16), key_grad.reshape(row_count, KVW).astype(jnp.bfloat16), value_grad.reshape(row_count, KVW).astype(jnp.bfloat16))

def section_sequence(hidden_seq, gain_row, weight, query_seq, key_seq, grad_seq):
    hidden_wide = hidden_seq.astype(jnp.float32)
    inv_rms = lax.rsqrt(lax.optimization_barrier(jnp.mean(hidden_wide * hidden_wide, axis=-1, keepdims=True)) + EPSILON)
    normalized = hidden_wide * inv_rms
    normed = (normalized * gain_row).astype(jnp.bfloat16)
    values = jnp.dot(normed, weight, preferred_element_type=jnp.float32).astype(jnp.bfloat16)
    query_grad, key_grad, value_grad = attend_back(query_seq, key_seq, values, grad_seq)
    normed_grad = jnp.dot(value_grad, weight.T, preferred_element_type=jnp.float32)
    gain_scaled = normed_grad * gain_row
    branch_grad = inv_rms * (gain_scaled - normalized * lax.optimization_barrier(jnp.mean(gain_scaled * normalized, axis=-1, keepdims=True)))
    weight_term = jnp.dot(normed.T, value_grad, preferred_element_type=jnp.float32)
    gain_term = lax.optimization_barrier(jnp.sum(normed_grad * normalized, axis=0))
    return (branch_grad, query_grad, key_grad, weight_term, gain_term)

def reference(hidden_in, query_rows, key_rows, context_grad, stream_top, norm_gain, value_weight):
    seq_count = TOKENS // TOK_DEV
    grad_scale = float(TOKENS) ** (-0.5)
    incoming = stream_top
    streams, queries, keys_out, weights_out, gains_out = ([], [], [], [], [])
    for section_number in range(SECTIONS - 1, -1, -1):
        gain_row = norm_gain[section_number].astype(jnp.float32)
        weight = value_weight[section_number]

        def per_sequence(totals, pieces):
            hidden_seq, query_seq, key_seq, grad_seq = pieces
            branch_grad, query_grad, key_grad, weight_term, gain_term = section_sequence(hidden_seq, gain_row, weight, query_seq, key_seq, grad_seq)
            return ((totals[0] + weight_term, totals[1] + gain_term), (branch_grad, query_grad, key_grad))
        zeros_init = (jnp.zeros((D, KVW), jnp.float32), jnp.zeros((D,), jnp.float32))
        pieces = (hidden_in[section_number].reshape(seq_count, TOK_DEV, D), query_rows[section_number].reshape(seq_count, TOK_DEV, QW), key_rows[section_number].reshape(seq_count, TOK_DEV, KVW), context_grad[section_number].reshape(seq_count, TOK_DEV, QW))
        (weight_sum, gain_sum), (branch_grad, query_grad, key_grad) = lax.scan(per_sequence, zeros_init, pieces)
        stream = (incoming.astype(jnp.float32) + branch_grad.reshape(TOKENS, D)).astype(jnp.bfloat16)
        incoming = stream
        streams.append(stream)
        queries.append(query_grad.reshape(TOKENS, QW))
        keys_out.append(key_grad.reshape(TOKENS, KVW))
        weights_out.append(weight_sum * grad_scale)
        gains_out.append(gain_sum * grad_scale)
    return (jnp.stack(streams[::-1]), jnp.stack(queries[::-1]), jnp.stack(keys_out[::-1]), jnp.stack(weights_out[::-1]), jnp.stack(gains_out[::-1]))
```

```python
import itertools

import jax
import jax.numpy as jnp
from jax import lax
from jax.experimental import pallas as pl
from jax.experimental.pallas import tpu as pltpu
from jax.sharding import PartitionSpec as P

D = 8192
HEAD = 128
QHEADS = 32
KV = 4
GROUP = QHEADS // KV
TOK = 128
KVW = KV * HEAD
BLK = 256
EPSILON = 1e-05
SCORE_SCALE = 1.0 / HEAD**0.5
GRAD_SCALE = 16384.0**-0.5
F32, BF16 = jnp.float32, jnp.bfloat16

ORDER = (
    (0, 0), (3, 0), (1, 0), (0, 3), (0, 1), (2, 0), (0, 2),
    (3, 3), (1, 3), (3, 1), (1, 1), (2, 3), (2, 1), (3, 2), (1, 2), (2, 2),
)
EARLY = 7
NSEM = 176


def dot(a, b):
    return jnp.dot(a, b, preferred_element_type=F32)


def dot_nt(a, b):
    return lax.dot_general(a, b, (((1,), (1,)), ((), ())), preferred_element_type=F32)


def kernel(
    hid_h, query_h, key_h, ctx_h, top_h, gain_h, w_h,
    stream_o, qg_o, kg_o, vwg_o, gg_o,
    hid, hsib, query, key, ctx, top, gain, gain1, inv, inv_sib, inv1, cen, cen1,
    w_all, w1, normed, vg, vg1, vgt, probs, vpart, vrecv, values,
    ng, ng_stage, ng1, ng1_stage, hid1, stream, late,
    wt, rbuf, fin, rep_stage, rep_recv, rep_all, wown, qg, kg, vwg, gg,
    ssem, rsem, lsem,
):
    pipe = lax.axis_index("pipe")
    rep = lax.axis_index("rep")
    shard = lax.axis_index("shard")
    core = lax.rem(shard, 2)
    chip = lax.div(shard, 2)
    x, y = lax.rem(chip, 4), lax.div(chip, 4)
    is_top = pipe == 1
    is_low = pipe == 0
    ids = itertools.count()
    local_ids = itertools.count()
    sent = []

    def chip_at(dx, dy):
        return lax.rem(y + dy % 4, 4) * 4 + lax.rem(x + dx % 4, 4)

    def peer(dx, dy):
        return {"shard": chip_at(dx, dy) * 2 + core}

    sibling = {"shard": chip * 2 + (1 - core)}
    below = {"pipe": 0}
    ahead = {"pipe": 0, "rep": lax.rem(rep + 1, 4)}

    def remote(src, dst, device, who=None):
        number = next(ids)
        copy = pltpu.make_async_remote_copy(
            src_ref=src, dst_ref=dst, send_sem=ssem.at[number], recv_sem=rsem.at[number],
            device_id=device, device_id_type=pl.DeviceIdType.MESH,
        )
        sent.append((copy, who))
        return copy

    def send(src, dst, device):
        copy = remote(src, dst, device)
        copy.start()
        return copy

    def local(src, dst):
        copy = pltpu.make_async_copy(src, dst, lsem.at[next(local_ids)])
        copy.start()
        return copy

    def cols(start, width):
        return pl.ds(pl.multiple_of(start, 128), width)

    load_hid = local(hid_h, hid)
    load_gain = local(gain_h, gain)
    load_key = local(key_h, key)
    load_query = local(query_h, query)
    load_ctx = local(ctx_h, ctx)
    load_w = local(w_h, w_all.at[chip])
    load_top = local(top_h, top)

    barrier = pltpu.get_barrier_semaphore()
    partners = [peer(1, 0), peer(3, 0), peer(0, 1), peer(0, 3), sibling, {"pipe": 1 - pipe}]
    partners += [{"rep": lax.rem(rep + o, 4)} for o in (1, 2, 3)]
    partners += [{"pipe": 1 - pipe, "rep": lax.rem(rep + jnp.where(is_top, 1, 3), 4)}]
    for device in partners:
        pl.semaphore_signal(barrier, inc=1, device_id=device, device_id_type=pl.DeviceIdType.MESH)
    pl.semaphore_wait(barrier, len(partners))

    def step(half, first, by):
        along_x = (half == 0) == first
        return (by, 0) if along_x else (0, by)

    def shift(half, first_by, second_by):
        return (first_by, second_by) if half == 0 else (second_by, first_by)

    def rows(half, quarter=None):
        if quarter is None:
            return pl.ds(half * 128, 128)
        return pl.ds(half * 128 + quarter * 64, 64)

    gather = {}

    def gather_own(half, first):
        for kind, by in ((0, 1), (1, 3)):
            src = w_h.at[rows(half), :]
            gather[half, first, 0, kind] = send(
                src, w_all.at[chip, rows(half), :], peer(*step(half, first, by))
            )

    def gather_pass(half, offset, index):
        j = chip_at(*shift(half, offset, 0))
        for kind, by in ((0, 1), (1, 3)):
            part = w_all.at[j, rows(half), :]
            gather[half, False, index, kind] = send(part, part, peer(*step(half, False, by)))

    def gather_forward(half, first, index, offset):
        for kind, by in ((0, 3), (1, 1)):
            gather[half, first, index, kind].wait_recv()
            move = shift(half, by, 0) if first else shift(half, offset, by)
            part = w_all.at[chip_at(*move), rows(half, kind), :]
            to = 1 if kind == 0 else 3
            gather[half, first, index, kind + 2] = send(part, part, peer(*step(half, first, to)))

    def gather_end(half, first, index):
        for kind in (2, 3):
            gather[half, first, index, kind].wait_recv()

    early = []
    for e in range(EARLY):
        j = chip_at(*ORDER[e])
        early.append((
            j,
            remote(hid_h.at[:, cols(j * 512, 512)], hid1.at[:, pl.ds(e * 512, 512)], below, "down"),
            remote(w_h if e == 0 else w_all.at[j], w1.at[e], ahead, "down"),
        ))
    send_gain1 = remote(gain_h, gain1, below, "down")

    for half in (0, 1):
        gather_own(half, True)
    for half in (0, 1):
        gather_own(half, False)
    hsib_copies = []
    for j in range(16):
        hsib_copies.append(send(
            hid_h.at[:, cols((2 * j + 1 - core) * BLK, BLK)], hsib.at[:, pl.ds(j * BLK, BLK)], sibling
        ))

    @pl.when(is_top)
    def _():
        early[0][2].start()
        send_gain1.start()
        for _, down, _ in early:
            down.start()

    load_hid.wait()
    load_gain.wait()

    def square(i, total):
        part = hid[:, cols(i * 512, 512)].astype(F32)
        part = part * part
        for n in range(4):
            total = total + part[:, n * 128:(n + 1) * 128]
        return total

    total = lax.fori_loop(0, 16, square, jnp.zeros((TOK, 128), F32))
    mean = jnp.sum(total, axis=1, keepdims=True) * (1.0 / D)
    inv[...] = jnp.broadcast_to(lax.rsqrt(mean + EPSILON), (TOK, 128))
    send_inv = send(inv, inv_sib, sibling)
    send_inv1 = remote(inv, inv1, below, "down")

    @pl.when(is_top)
    def _():
        send_inv1.start()

    load_key.wait()
    load_query.wait()
    load_ctx.wait()

    def stacked(ref, k):
        return jnp.concatenate(
            [ref[:, (GROUP * k + g) * HEAD:(GROUP * k + g + 1) * HEAD] for g in range(GROUP)], axis=0
        )

    def attend(k):
        lanes = slice(k * HEAD, (k + 1) * HEAD)
        scores = dot_nt(key[:, lanes], stacked(query, k)) * SCORE_SCALE
        u = lax.broadcasted_iota(jnp.int32, scores.shape, 0)
        t = lax.broadcasted_iota(jnp.int32, scores.shape, 1) & (TOK - 1)
        scores = jnp.where(u <= t, scores, -1e30)
        raw = jnp.exp(scores - jnp.max(scores, axis=0, keepdims=True))
        prob = raw / jnp.sum(raw, axis=0, keepdims=True)
        probs[k] = prob
        vg[0:TOK, lanes] = dot(prob.astype(BF16), stacked(ctx, k)).astype(BF16)

    attend(0)
    for half in (0, 1):
        gather_forward(half, True, 0, 0)
        gather_pass(half, 3, 1)
        gather_pass(half, 1, 2)
    attend(1)
    for half in (0, 1):
        gather_forward(half, False, 0, 0)
    load_w.wait()

    @pl.when(is_top)
    def _():
        for e in range(1, 5):
            early[e][2].start()

    attend(2)
    for half in (0, 1):
        gather_end(half, True, 0)
        gather_pass(half, 2, 3)
    attend(3)

    send_vg = send(vg.at[pl.ds(0, TOK), :], vg.at[pl.ds(TOK, TOK), :], sibling)
    send_vg1 = remote(vg.at[pl.ds(0, TOK), :], vg1.at[pl.ds(0, TOK), :], below, "down")

    @pl.when(is_top)
    def _():
        send_vg1.start()

    for half in (0, 1):
        gather_end(half, False, 0)

    @pl.when(is_top)
    def _():
        for e in range(5, 7):
            early[e][2].start()

    for copy in hsib_copies:
        copy.wait_recv()
    send_inv.wait_recv()

    def norm_block(j, carry):
        gain_row = gain[:, cols((2 * j + core) * BLK, BLK)]
        own = hid[:, cols((2 * j + core) * BLK, BLK)].astype(F32) * inv[:, 0:1]
        other = hsib[:, cols(j * BLK, BLK)].astype(F32) * inv_sib[:, 0:1]
        normed[0:TOK, cols(j * BLK, BLK)] = (own * gain_row).astype(BF16)
        normed[TOK:, cols(j * BLK, BLK)] = (other * gain_row).astype(BF16)
        return carry

    lax.fori_loop(0, 16, norm_block, 0)
    for half in (0, 1):
        gather_forward(half, False, 1, 3)
        gather_forward(half, False, 2, 1)

    send_vg.wait_recv()
    vgt[...] = vg[...].astype(F32).T.astype(BF16)

    def weight_block(j, carry):
        wt[j] = dot(vgt[...], normed[:, cols(j * BLK, BLK)]).astype(BF16)
        return carry

    ng_copies = []

    def value_block(place):
        j = chip_at(*ORDER[place])
        block = w_all[j]
        part = dot(normed[:, cols(j * BLK, BLK)], block)
        if place == 0:
            vpart[...] = part
        else:
            vpart[...] += part
        grad = dot_nt(vg[...], block)
        where = cols((2 * j + core) * BLK, BLK)
        ng[:, where] = grad[0:TOK].astype(BF16)
        ng_stage[place] = grad[TOK:].astype(BF16)
        ng_copies.append(send(ng_stage.at[place], ng.at[:, where], sibling))

    for place in range(0, 4):
        value_block(place)
    for half in (0, 1):
        gather_forward(half, False, 3, 2)
    for place in range(4, 11):
        value_block(place)
    for half in (0, 1):
        gather_end(half, False, 1)
        gather_end(half, False, 2)
    for place in range(11, 15):
        value_block(place)
    lax.fori_loop(0, 16, weight_block, 0)
    for half in (0, 1):
        gather_end(half, False, 3)
    value_block(15)
    send_part = send(vpart.at[pl.ds(TOK, TOK), :], vrecv, sibling)

    def wrows(half, quarter):
        return pl.ds(half * 256 + quarter * 128, 128)

    scatter = {}

    def place_of(half, line, by):
        move = shift(half, by, line) if line < 4 else shift(half, 0, by)
        return chip_at(*move)

    def scatter_send(half, line, kind, by, quarter, to):
        scatter[half, line, kind] = send(
            wt.at[place_of(half, line, by), wrows(half, quarter), :],
            rbuf.at[half * 5 + line, kind],
            peer(*step(half, line < 4, to)),
        )

    def scatter_far(half, line):
        scatter_send(half, line, 0, 2, 0, 1)
        scatter_send(half, line, 1, 2, 1, 3)

    def scatter_near(half, line):
        scatter_send(half, line, 2, 1, 1, 1)
        scatter_send(half, line, 3, 3, 0, 3)

    def add_in(half, line, by, quarter, kinds):
        j = place_of(half, line, by)
        total = wt[j, wrows(half, quarter), :].astype(F32)
        for kind in kinds:
            total = total + rbuf[half * 5 + line, kind].astype(F32)
        return j, total

    def scatter_forward(half, line):
        for kind, by, quarter in ((0, 1, 0), (1, 3, 1)):
            scatter[half, line, kind].wait_recv()
            j, total = add_in(half, line, by, quarter, (kind,))
            wt[j, wrows(half, quarter), :] = total.astype(BF16)
            scatter_send(half, line, kind + 4, by, quarter, by)

    def scatter_own(half, line):
        for kind in (2, 3, 4, 5):
            scatter[half, line, kind].wait_recv()
        for quarter, kinds in ((0, (3, 4)), (1, (2, 5))):
            j, total = add_in(half, line, 0, quarter, kinds)
            if line < 4:
                wt[j, wrows(half, quarter), :] = total.astype(BF16)
            else:
                fin[wrows(half, quarter), :] = total

    lines = (2, 1, 3, 0)
    for line in lines:
        for half in (0, 1):
            scatter_far(half, line)
    for line in lines:
        for half in (0, 1):
            scatter_near(half, line)

    send_part.wait_recv()
    whole = vpart[0:TOK, :] + vrecv[...]
    values[...] = whole.astype(BF16)
    mean = jnp.sum(whole * vg[0:TOK, :].astype(F32), axis=1, keepdims=True) * (1.0 / D)
    cen[...] = jnp.broadcast_to(mean, (TOK, 128))
    send_cen1 = remote(cen, cen1, below, "down")

    for copy in ng_copies:
        copy.wait_recv()
    load_top.wait()

    def branch(hidden, scale, grad, gain_row, center):
        factor = scale[:, 0:1]
        normalized = hidden.astype(F32) * factor
        return factor * (grad.astype(F32) * gain_row - normalized * center[:, 0:1])

    def own_branch(where):
        return branch(hid[:, where], inv, ng[:, where], gain[:, where], cen)

    lates = []
    for e in range(EARLY, 16):
        j = chip_at(*ORDER[e])
        where = cols(j * 512, 512)
        lates.append((j, remote(
            stream.at[:, where], late.at[:, pl.ds((e - EARLY) * 512, 512)], below, "down"
        )))
    outs = [
        pltpu.make_async_copy(
            stream.at[:, pl.ds(n * 512, 512)], stream_o.at[:, pl.ds(n * 512, 512)], lsem.at[next(local_ids)]
        )
        for n in range(16)
    ]

    def top_block(j):
        where = cols(j * 512, 512)
        stream[:, where] = (top[:, where].astype(F32) + own_branch(where)).astype(BF16)

    @pl.when(is_top)
    def _():
        send_cen1.start()
        for j, copy in lates:
            top_block(j)
            copy.start()

    for half in (0, 1):
        scatter_forward(half, 2)

    def attend_back(k):
        lanes = slice(k * HEAD, (k + 1) * HEAD)
        queries, grads = stacked(query, k), stacked(ctx, k)
        prob = probs[k]
        grad_prob = dot_nt(values[:, lanes], grads)
        row_dot = jnp.sum(prob * grad_prob, axis=0, keepdims=True)
        wide = prob * (grad_prob - row_dot) * SCORE_SCALE
        grad_score = wide.astype(BF16)
        kg[:, lanes] = dot(grad_score, queries).astype(BF16)
        for g in range(GROUP):
            turned = wide[:, g * HEAD:(g + 1) * HEAD].T.astype(BF16)
            head = (GROUP * k + g) * HEAD
            qg[:, head:head + HEAD] = dot(turned, key[:, lanes]).astype(BF16)

    attend_back(0)
    for line in (1, 3):
        for half in (0, 1):
            scatter_forward(half, line)
    attend_back(1)
    for half in (0, 1):
        scatter_forward(half, 0)
        scatter_own(half, 2)
        scatter_far(half, 4)
    attend_back(2)
    for half in (0, 1):
        scatter_own(half, 1)
        scatter_own(half, 3)
        scatter_near(half, 4)
    attend_back(3)
    out_qg = local(qg, qg_o)
    out_kg = local(kg, kg_o)
    for half in (0, 1):
        scatter_own(half, 0)
        scatter_forward(half, 4)

    ng1_copies = []
    forward_vg1 = remote(vg1.at[pl.ds(0, TOK), :], vg1.at[pl.ds(TOK, TOK), :], sibling, "low")
    for e in range(EARLY):
        where = cols(e * 512 + core * BLK, BLK)
        ng1_copies.append(remote(ng1_stage.at[e], ng1.at[:, where], sibling, "low"))

    @pl.when(is_low)
    def _():
        send_vg1.wait_recv()
        forward_vg1.start()
        forward_vg1.wait_recv()
        for e in range(EARLY):
            early[e][2].wait_recv()
            grad = dot_nt(vg1[...], w1[e])
            ng1[:, cols(e * 512 + core * BLK, BLK)] = grad[0:TOK].astype(BF16)
            ng1_stage[e] = grad[TOK:].astype(BF16)
            ng1_copies[e].start()
        send_inv1.wait_recv()
        send_gain1.wait_recv()
        send_cen1.wait_recv()
        for e in range(EARLY):
            ng1_copies[e].wait_recv()
            early[e][1].wait_recv()
            here = pl.ds(e * 512, 512)
            where = cols(early[e][0] * 512, 512)
            upper = branch(hid1[:, here], inv1, ng1[:, here], gain1[:, where], cen1)
            upper = (top[:, where].astype(F32) + upper).astype(BF16)
            stream[:, where] = (upper.astype(F32) + own_branch(where)).astype(BF16)

    @pl.when(is_top)
    def _():
        for j, _, _ in early:
            top_block(j)

    for half in (0, 1):
        scatter_own(half, 4)

    for o in (1, 2, 3):
        q = lax.rem(rep + o, 4)
        rep_stage[o] = fin[pl.ds(pl.multiple_of(q * 128, 128), 128), :].astype(BF16)
    rep_copies = [
        send(rep_stage.at[o], rep_recv.at[o - 1], {"rep": lax.rem(rep + o, 4)}) for o in (1, 2, 3)
    ]
    mine = pl.ds(pl.multiple_of(rep * 128, 128), 128)
    wown[...] = w_all[chip].astype(F32).T
    total = fin[mine, :]
    for o in (1, 2, 3):
        rep_copies[o - 1].wait_recv()
        total = total + rep_recv[o - 1].astype(F32)
    rep_all[rep] = total.astype(BF16)
    all_copies = [
        send(rep_all.at[rep], rep_all.at[rep], {"rep": lax.rem(rep + o, 4)}) for o in (1, 2, 3)
    ]

    @pl.when(is_low)
    def _():
        for e, (j, copy) in enumerate(lates):
            copy.wait_recv()
            where = cols(j * 512, 512)
            upper = late[:, pl.ds(e * 512, 512)].astype(F32)
            stream[:, where] = (upper + own_branch(where)).astype(BF16)

    for copy in outs:
        copy.start()
    for copy in all_copies:
        copy.wait_recv()
    summed = jnp.concatenate([rep_all[q].astype(F32) for q in range(4)], axis=0) * GRAD_SCALE
    vwg[...] = summed.T
    gain_own = gain[:, cols(shard * BLK, BLK)]
    gg[...] = jnp.sum(summed * wown[...], axis=0, keepdims=True) / gain_own
    ends = [local(vwg, vwg_o), local(gg, gg_o), out_qg, out_kg] + outs
    for copy in ends:
        copy.wait()

    for copy, who in sent:
        if who is None:
            copy.wait_send()

    @pl.when(is_top)
    def _():
        for copy, who in sent:
            if who == "down":
                copy.wait_send()

    @pl.when(is_low)
    def _():
        for copy, who in sent:
            if who == "low":
                copy.wait_send()


def per_device(hidden_in, query_rows, key_rows, context_grad, stream_top, norm_gain, value_weight):
    def vmem(*shape, dtype=BF16):
        return pltpu.VMEM(shape, dtype)

    scratch = [
        vmem(TOK, D), vmem(TOK, D // 2), vmem(TOK, 4096), vmem(TOK, KVW), vmem(TOK, 4096), vmem(TOK, D),
        vmem(1, D, dtype=F32), vmem(1, D, dtype=F32),
        *[vmem(TOK, 128, dtype=F32) for _ in range(5)],
        vmem(16, BLK, KVW), vmem(EARLY, BLK, KVW), vmem(2 * TOK, 4096),
        vmem(2 * TOK, KVW), vmem(2 * TOK, KVW), vmem(KVW, 2 * TOK),
        vmem(KV, TOK, GROUP * TOK, dtype=F32),
        vmem(2 * TOK, KVW, dtype=F32), vmem(TOK, KVW, dtype=F32), vmem(TOK, KVW),
        vmem(TOK, D), vmem(16, TOK, BLK), vmem(TOK, EARLY * 512), vmem(EARLY, TOK, BLK),
        vmem(TOK, EARLY * 512), vmem(TOK, D), vmem(TOK, (16 - EARLY) * 512),
        vmem(16, KVW, BLK), vmem(10, 6, 128, BLK), vmem(KVW, BLK, dtype=F32),
        vmem(4, 128, BLK), vmem(3, 128, BLK), vmem(4, 128, BLK), vmem(KVW, BLK, dtype=F32),
        vmem(TOK, 4096), vmem(TOK, KVW), vmem(BLK, KVW, dtype=F32), vmem(1, BLK, dtype=F32),
        pltpu.SemaphoreType.DMA((NSEM,)), pltpu.SemaphoreType.DMA((NSEM,)), pltpu.SemaphoreType.DMA((32,)),
    ]
    outs = pl.pallas_call(
        kernel,
        out_shape=(
            jax.ShapeDtypeStruct((TOK, D), BF16),
            jax.ShapeDtypeStruct((TOK, 4096), BF16),
            jax.ShapeDtypeStruct((TOK, KVW), BF16),
            jax.ShapeDtypeStruct((BLK, KVW), F32),
            jax.ShapeDtypeStruct((1, BLK), F32),
        ),
        in_specs=[pl.BlockSpec(memory_space=pl.ANY)] * 7,
        out_specs=[pl.BlockSpec(memory_space=pl.ANY)] * 5,
        scratch_shapes=scratch,
        compiler_params=pltpu.CompilerParams(
            collective_id=0, has_side_effects=True, vmem_limit_bytes=56 * 1024 * 1024
        ),
        cost_estimate=pl.CostEstimate(flops=5 * 10**9, bytes_accessed=12 * 10**6, transcendentals=10**6),
    )(hidden_in[0], query_rows[0], key_rows[0], context_grad[0], stream_top, norm_gain, value_weight[0])
    stream, query_grad, key_grad, weight_grad, gain_grad = outs
    return stream[None], query_grad[None], key_grad[None], weight_grad[None], gain_grad


def solution(mesh):
    return jax.shard_map(
        per_device,
        mesh=mesh,
        in_specs=(
            P("pipe", ("rep", "shard"), None),
            P("pipe", ("rep", "shard"), None),
            P("pipe", ("rep", "shard"), None),
            P("pipe", ("rep", "shard"), None),
            P(("rep", "shard"), None),
            P("pipe", None),
            P("pipe", "shard", None),
        ),
        out_specs=(
            P("pipe", ("rep", "shard"), None),
            P("pipe", ("rep", "shard"), None),
            P("pipe", ("rep", "shard"), None),
            P("pipe", "shard", None),
            P("pipe", "shard"),
        ),
        check_vma=False,
    )
```

```python
import itertools

import jax
import jax.numpy as jnp
from jax import lax
from jax.experimental import pallas as pl
from jax.experimental.pallas import tpu as pltpu
from jax.sharding import PartitionSpec as P

D = 8192
HEAD = 128
QHEADS = 32
KV = 4
GROUP = QHEADS // KV
TOK = 128
KVW = KV * HEAD
BLK = 256
EPSILON = 1e-05
SCORE_SCALE = 1.0 / HEAD**0.5
GRAD_SCALE = 16384.0**-0.5
F32, BF16 = jnp.float32, jnp.bfloat16

ORDER = (
    (0, 0), (3, 0), (1, 0), (0, 3), (0, 1), (2, 0), (0, 2),
    (3, 3), (1, 3), (3, 1), (1, 1), (2, 3), (2, 1), (3, 2), (1, 2), (2, 2),
)
EARLY = 8
NSEM = 228 + 3 * EARLY


def dot(a, b):
    return jnp.dot(a, b, preferred_element_type=F32)


def dot_nt(a, b):
    return lax.dot_general(a, b, (((1,), (1,)), ((), ())), preferred_element_type=F32)


def kernel(
    hid_h, query_h, key_h, ctx_h, top_h, gain_h, w_h,
    stream, qg, kg, vwg, gg,
    hid, hsib, query, key, ctx, top, gain, gain1, inv, inv_sib, inv1, cen, cen1,
    inv_row, inv1_row, cen_row, cen1_row,
    w_all, w1, normed, vg, vg1, vgt, probs, vpart, vrecv, values,
    ng, ng_stage, ng1, ng1_stage, hid1, late, own,
    wt, rbuf, fin, rep_stage, rep_recv, rep_all, wown,
    ssem, rsem, lsem,
):
    pipe = lax.axis_index("pipe")
    rep = lax.axis_index("rep")
    shard = lax.axis_index("shard")
    core = lax.rem(shard, 2)
    chip = lax.div(shard, 2)
    x, y = lax.rem(chip, 4), lax.div(chip, 4)
    is_top = pipe == 1
    is_low = pipe == 0
    ids = itertools.count()
    local_ids = itertools.count()
    sent = []

    def chip_at(dx, dy):
        return lax.rem(y + dy % 4, 4) * 4 + lax.rem(x + dx % 4, 4)

    def peer(dx, dy):
        return {"shard": chip_at(dx, dy) * 2 + core}

    sibling = {"shard": chip * 2 + (1 - core)}
    below = {"pipe": 0}
    ahead = {"pipe": 0, "rep": lax.rem(rep + 1, 4)}

    def remote(src, dst, device, who=None):
        number = next(ids)
        copy = pltpu.make_async_remote_copy(
            src_ref=src, dst_ref=dst, send_sem=ssem.at[number], recv_sem=rsem.at[number],
            device_id=device, device_id_type=pl.DeviceIdType.MESH,
        )
        sent.append((copy, who))
        return copy

    def send(src, dst, device):
        copy = remote(src, dst, device)
        copy.start()
        return copy

    def local(src, dst):
        copy = pltpu.make_async_copy(src, dst, lsem.at[next(local_ids)])
        copy.start()
        return copy

    def cols(start, width):
        return pl.ds(pl.multiple_of(start, 128), width)

    load_hid = local(hid_h, hid)
    load_gain = local(gain_h, gain)
    load_key = local(key_h, key)
    load_query = local(query_h, query)
    load_ctx = local(ctx_h, ctx)
    load_w = local(w_h, w_all.at[chip])
    load_top = local(top_h, top)

    barrier = pltpu.get_barrier_semaphore()
    partners = [peer(1, 0), peer(3, 0), peer(0, 1), peer(0, 3), sibling, {"pipe": 1 - pipe}]
    partners += [{"rep": lax.rem(rep + o, 4)} for o in (1, 2, 3)]
    partners += [{"pipe": 1 - pipe, "rep": lax.rem(rep + jnp.where(is_top, 1, 3), 4)}]
    for device in partners:
        pl.semaphore_signal(barrier, inc=1, device_id=device, device_id_type=pl.DeviceIdType.MESH)
    pl.semaphore_wait(barrier, len(partners))

    def step(half, first, by):
        along_x = (half == 0) == first
        return (by, 0) if along_x else (0, by)

    def shift(half, first_by, second_by):
        return (first_by, second_by) if half == 0 else (second_by, first_by)

    def rows(half, quarter=None):
        if quarter is None:
            return pl.ds(half * 128, 128)
        return pl.ds(half * 128 + quarter * 64, 64)

    gather = {}

    def gather_own(half, first):
        for kind, by in ((0, 1), (1, 3)):
            src = w_h.at[rows(half), :]
            gather[half, first, 0, kind] = send(
                src, w_all.at[chip, rows(half), :], peer(*step(half, first, by))
            )

    def gather_pass(half, offset, index):
        j = chip_at(*shift(half, offset, 0))
        for kind, by in ((0, 1), (1, 3)):
            part = w_all.at[j, rows(half), :]
            gather[half, False, index, kind] = send(part, part, peer(*step(half, False, by)))

    def gather_forward(half, first, index, offset):
        for kind, by in ((0, 3), (1, 1)):
            gather[half, first, index, kind].wait_recv()
            move = shift(half, by, 0) if first else shift(half, offset, by)
            part = w_all.at[chip_at(*move), rows(half, kind), :]
            to = 1 if kind == 0 else 3
            gather[half, first, index, kind + 2] = send(part, part, peer(*step(half, first, to)))

    def gather_end(half, first, index):
        for kind in (2, 3):
            gather[half, first, index, kind].wait_recv()

    early = []
    for e in range(EARLY):
        j = chip_at(*ORDER[e])
        early.append((
            j,
            remote(hid_h.at[:, cols(j * 512, 512)], hid1.at[:, pl.ds(e * 512, 512)], below, "down"),
            [
                remote((w_h if e == 0 else w_all.at[j]).at[rows(half), :], w1.at[e, rows(half), :], ahead, "down")
                for half in (0, 1)
            ],
        ))
    send_gain1 = remote(gain_h, gain1, below, "down")

    for half in (0, 1):
        gather_own(half, True)
    for half in (0, 1):
        gather_own(half, False)
    hsib_copies = []
    for j in range(16):
        hsib_copies.append(send(
            hid_h.at[:, cols((2 * j + 1 - core) * BLK, BLK)], hsib.at[:, pl.ds(j * BLK, BLK)], sibling
        ))

    @pl.when(is_top)
    def _():
        early[0][2][0].start()
        early[0][2][1].start()
        send_gain1.start()
        for _, down, _ in early:
            down.start()

    load_hid.wait()
    load_gain.wait()

    def square(i, total):
        part = hid[:, cols(i * 512, 512)].astype(F32)
        part = part * part
        for n in range(4):
            total = total + part[:, n * 128:(n + 1) * 128]
        return total

    total = lax.fori_loop(0, 16, square, jnp.zeros((TOK, 128), F32))
    mean = jnp.sum(total, axis=1, keepdims=True) * (1.0 / D)
    inv[...] = jnp.broadcast_to(lax.rsqrt(mean + EPSILON), (TOK, 128))
    send_inv = send(inv, inv_sib, sibling)
    inv_row[...] = inv[...].T[0:8, :]
    send_inv1 = remote(inv_row, inv1_row, below, "down")

    @pl.when(is_top)
    def _():
        send_inv1.start()

    load_key.wait()
    load_query.wait()
    load_ctx.wait()

    def stacked(ref, k):
        return jnp.concatenate(
            [ref[:, (GROUP * k + g) * HEAD:(GROUP * k + g + 1) * HEAD] for g in range(GROUP)], axis=0
        )

    def attend(k):
        lanes = slice(k * HEAD, (k + 1) * HEAD)
        scores = dot_nt(key[:, lanes], stacked(query, k)) * SCORE_SCALE
        u = lax.broadcasted_iota(jnp.int32, scores.shape, 0)
        t = lax.broadcasted_iota(jnp.int32, scores.shape, 1) & (TOK - 1)
        scores = jnp.where(u <= t, scores, -1e30)
        raw = jnp.exp(scores - jnp.max(scores, axis=0, keepdims=True))
        prob = raw / jnp.sum(raw, axis=0, keepdims=True)
        probs[k] = prob
        vg[0:TOK, lanes] = dot(prob.astype(BF16), stacked(ctx, k)).astype(BF16)

    attend(0)
    for half in (0, 1):
        gather_forward(half, True, 0, 0)
        gather_pass(half, 3, 1)
        gather_pass(half, 1, 2)

    @pl.when(is_top)
    def _():
        for e, half in ((1, 0), (2, 0), (3, 1), (4, 1)):
            early[e][2][half].start()

    attend(1)
    for half in (0, 1):
        gather_forward(half, False, 0, 0)
    load_w.wait()

    @pl.when(is_top)
    def _():
        for e, half in ((1, 1), (2, 1), (3, 0), (4, 0)):
            early[e][2][half].start()

    attend(2)
    for half in (0, 1):
        gather_end(half, True, 0)
        gather_pass(half, 2, 3)
    attend(3)

    send_vg = send(vg.at[pl.ds(0, TOK), :], vg.at[pl.ds(TOK, TOK), :], sibling)
    send_vg1 = remote(vg.at[pl.ds(0, TOK), :], vg1.at[pl.ds(0, TOK), :], below, "down")

    @pl.when(is_top)
    def _():
        send_vg1.start()

    for half in (0, 1):
        gather_end(half, False, 0)

    @pl.when(is_top)
    def _():
        for e in range(5, 7):
            for half in (0, 1):
                early[e][2][half].start()

    for copy in hsib_copies:
        copy.wait_recv()
    send_inv.wait_recv()

    def norm_block(j, carry):
        gain_row = gain[:, cols((2 * j + core) * BLK, BLK)]
        own = hid[:, cols((2 * j + core) * BLK, BLK)].astype(F32) * inv[:, 0:1]
        other = hsib[:, cols(j * BLK, BLK)].astype(F32) * inv_sib[:, 0:1]
        normed[0:TOK, cols(j * BLK, BLK)] = (own * gain_row).astype(BF16)
        normed[TOK:, cols(j * BLK, BLK)] = (other * gain_row).astype(BF16)
        return carry

    lax.fori_loop(0, 16, norm_block, 0)
    for half in (0, 1):
        gather_forward(half, False, 1, 3)
        gather_forward(half, False, 2, 1)

    send_vg.wait_recv()
    vgt[...] = vg[...].astype(F32).T.astype(BF16)

    def weight_block(j, carry):
        wt[j] = dot(vgt[...], normed[:, cols(j * BLK, BLK)]).astype(BF16)
        return carry

    ng_copies = []

    def value_block(place):
        j = chip_at(*ORDER[place])
        block = w_all[j]
        part = dot(normed[:, cols(j * BLK, BLK)], block)
        if place == 0:
            vpart[...] = part
        else:
            vpart[...] += part
        grad = dot_nt(vg[...], block)
        where = cols((2 * j + core) * BLK, BLK)
        ng[:, where] = grad[0:TOK].astype(BF16)
        ng_stage[place] = grad[TOK:].astype(BF16)
        ng_copies.append(send(ng_stage.at[place], ng.at[:, where], sibling))

    @pl.when(is_top)
    def _():
        for e in range(7, EARLY):
            for half in (0, 1):
                early[e][2][half].start()

    def wrows(half, quarter):
        return pl.ds(half * 256 + quarter * 128, 128)

    scatter = {}

    def place_of(half, line, by):
        move = shift(half, by, line) if line < 4 else shift(half, 0, by)
        return chip_at(*move)

    def lanes_of(wave):
        return pl.ds(wave * 128, 128)

    def scatter_make(wave, half, line, kind, by, quarter, to):
        scatter[wave, half, line, kind] = remote(
            wt.at[place_of(half, line, by), wrows(half, quarter), lanes_of(wave)],
            rbuf.at[wave * 10 + half * 5 + line, kind],
            peer(*step(half, line < 4, to)),
        )
        return scatter[wave, half, line, kind]

    def scatter_send(*what):
        scatter_make(*what).start()

    def scatter_far(wave, line):
        for half in (0, 1):
            scatter_send(wave, half, line, 0, 2, 0, 1)
            scatter_send(wave, half, line, 1, 2, 1, 3)

    def scatter_near(wave, line):
        for half in (0, 1):
            scatter_send(wave, half, line, 2, 1, 1, 1)
            scatter_send(wave, half, line, 3, 3, 0, 3)

    def add_in(wave, half, line, by, quarter, kinds):
        j = place_of(half, line, by)
        total = wt[j, wrows(half, quarter), lanes_of(wave)].astype(F32)
        for kind in kinds:
            total = total + rbuf[wave * 10 + half * 5 + line, kind].astype(F32)
        return j, total

    def scatter_forward(wave, line):
        for half in (0, 1):
            for kind, by, quarter in ((0, 1, 0), (1, 3, 1)):
                scatter[wave, half, line, kind].wait_recv()
                j, total = add_in(wave, half, line, by, quarter, (kind,))
                wt[j, wrows(half, quarter), lanes_of(wave)] = total.astype(BF16)
                scatter_send(wave, half, line, kind + 4, by, quarter, by)

    def scatter_own(wave, line):
        for half in (0, 1):
            for kind in (2, 3, 4, 5):
                scatter[wave, half, line, kind].wait_recv()
            for quarter, kinds in ((0, (3, 4)), (1, (2, 5))):
                j, total = add_in(wave, half, line, 0, quarter, kinds)
                if line < 4:
                    wt[j, wrows(half, quarter), lanes_of(wave)] = total.astype(BF16)
                else:
                    fin[wave, half * 2 + quarter] = total

    rep_copies = {}

    def rep_first(wave):
        for o in (1, 2, 3):
            q = lax.rem(rep + o, 4)
            rep_stage[wave, o] = fin[wave, q].astype(BF16)
            rep_copies[wave, o] = send(rep_stage.at[wave, o], rep_recv.at[wave, o - 1], {"rep": q})

    def rep_second(wave):
        total = fin[wave, rep]
        for o in (1, 2, 3):
            rep_copies[wave, o].wait_recv()
            total = total + rep_recv[wave, o - 1].astype(F32)
        rep_all[wave, rep] = total.astype(BF16)
        for o in (1, 2, 3):
            here = rep_all.at[wave, rep]
            rep_copies[wave, o + 3] = send(here, here, {"rep": lax.rem(rep + o, 4)})

    def scatter_start(wave):
        for line in (2, 1, 3, 0):
            scatter_far(wave, line)

    def scatter_start_near(wave):
        for line in (2, 1, 3, 0):
            scatter_near(wave, line)

    def scatter_stage(wave, stage):
        if stage == 0:
            scatter_forward(wave, 2)
        elif stage == 1:
            scatter_forward(wave, 1)
            scatter_forward(wave, 3)
        elif stage == 2:
            scatter_forward(wave, 0)
            scatter_own(wave, 2)
            scatter_far(wave, 4)
        elif stage == 3:
            scatter_own(wave, 1)
            scatter_own(wave, 3)
            scatter_near(wave, 4)
        elif stage == 4:
            scatter_own(wave, 0)
            scatter_forward(wave, 4)
        elif stage == 5:
            scatter_own(wave, 4)
            rep_first(wave)
        else:
            rep_second(wave)

    opening = []
    for line in (2, 1, 3, 0):
        for half in (0, 1):
            opening.append(scatter_make(0, half, line, 0, 2, 0, 1))
            opening.append(scatter_make(0, half, line, 1, 2, 1, 3))
    for line in (2, 1, 3, 0):
        for half in (0, 1):
            opening.append(scatter_make(0, half, line, 2, 1, 1, 1))
            opening.append(scatter_make(0, half, line, 3, 3, 0, 3))

    def open_scatter():
        lax.fori_loop(0, 16, weight_block, 0)
        for copy in opening:
            copy.start()

    pl.when(is_low)(open_scatter)

    for place in range(0, 7):
        value_block(place)
    for half in (0, 1):
        gather_forward(half, False, 3, 2)
    for place in range(7, 11):
        value_block(place)
    for half in (0, 1):
        gather_end(half, False, 1)
        gather_end(half, False, 2)
    for place in range(11, 15):
        value_block(place)
    for half in (0, 1):
        gather_end(half, False, 3)
    value_block(15)
    send_part = send(vpart.at[pl.ds(TOK, TOK), :], vrecv, sibling)
    pl.when(is_top)(open_scatter)

    send_part.wait_recv()
    whole = vpart[0:TOK, :] + vrecv[...]
    values[...] = whole.astype(BF16)
    mean = jnp.sum(whole * vg[0:TOK, :].astype(F32), axis=1, keepdims=True) * (1.0 / D)
    cen[...] = jnp.broadcast_to(mean, (TOK, 128))
    cen_row[...] = cen[...].T[0:8, :]
    send_cen1 = remote(cen_row, cen1_row, below, "down")

    for copy in ng_copies:
        copy.wait_recv()
    load_top.wait()

    def branch(hidden, scale, grad, gain_row, center):
        factor = scale[:, 0:1]
        normalized = hidden.astype(F32) * factor
        return factor * (grad.astype(F32) * gain_row - normalized * center[:, 0:1])

    def own_branch(where):
        return branch(hid[:, where], inv, ng[:, where], gain[:, where], cen)

    lates = []
    for e in range(EARLY, 16):
        j = chip_at(*ORDER[e])
        where = cols(j * 512, 512)
        lates.append((j, remote(
            stream.at[:, where], late.at[:, pl.ds((e - EARLY) * 512, 512)], below, "down"
        )))
    def top_block(j):
        where = cols(j * 512, 512)
        stream[:, where] = (top[:, where].astype(F32) + own_branch(where)).astype(BF16)

    def send_lates(start, stop):
        @pl.when(is_top)
        def _():
            if start == 0:
                send_cen1.start()
            for j, copy in lates[start:stop]:
                top_block(j)
                copy.start()

        @pl.when(is_low)
        def _():
            for n in range(2 * start, 2 * stop):
                where = pl.ds(n * 512, 512)
                own[:, where] = own_branch(where)

    def top_early(start, stop):
        @pl.when(is_top)
        def _():
            for j, _, _ in early[start:stop]:
                top_block(j)

    send_lates(0, 2)
    scatter_stage(0, 0)
    scatter_stage(0, 1)
    scatter_start(1)
    send_lates(2, 3)
    scatter_stage(0, 2)
    scatter_start_near(1)
    send_lates(3, 4)
    scatter_stage(0, 3)
    scatter_stage(1, 0)
    send_lates(4, 5)

    def attend_back(k):
        lanes = slice(k * HEAD, (k + 1) * HEAD)
        queries, grads = stacked(query, k), stacked(ctx, k)
        prob = probs[k]
        grad_prob = dot_nt(values[:, lanes], grads)
        row_dot = jnp.sum(prob * grad_prob, axis=0, keepdims=True)
        wide = prob * (grad_prob - row_dot) * SCORE_SCALE
        grad_score = wide.astype(BF16)
        kg[:, lanes] = dot(grad_score, queries).astype(BF16)
        for g in range(GROUP):
            turned = wide[:, g * HEAD:(g + 1) * HEAD].T.astype(BF16)
            head = (GROUP * k + g) * HEAD
            qg[:, head:head + HEAD] = dot(turned, key[:, lanes]).astype(BF16)

    ng1_copies = []
    forward_vg1 = remote(vg1.at[pl.ds(0, TOK), :], vg1.at[pl.ds(TOK, TOK), :], sibling, "low")
    for e in range(EARLY):
        where = cols(e * 512 + core * BLK, BLK)
        ng1_copies.append(remote(ng1_stage.at[e], ng1.at[:, where], sibling, "low"))

    @pl.when(is_low)
    def _():
        send_vg1.wait_recv()
        forward_vg1.start()

    def early_grads(start, stop):
        @pl.when(is_low)
        def _():
            if start == 0:
                forward_vg1.wait_recv()
            for e in range(start, stop):
                for half in (0, 1):
                    early[e][2][half].wait_recv()
                grad = dot_nt(vg1[...], w1[e])
                ng1[:, cols(e * 512 + core * BLK, BLK)] = grad[0:TOK].astype(BF16)
                ng1_stage[e] = grad[TOK:].astype(BF16)
                ng1_copies[e].start()

    wown[...] = w_all[chip].astype(F32).T

    def finish(wave):
        for o in (4, 5, 6):
            rep_copies[wave, o].wait_recv()
        summed = jnp.concatenate([rep_all[wave, q].astype(F32) for q in range(4)], axis=0) * GRAD_SCALE
        here = slice(wave * 128, wave * 128 + 128)
        vwg[here, :] = summed.T
        gain_own = gain[:, cols(shard * BLK + wave * 128, 128)]
        gg[:, here] = jnp.sum(summed * wown[:, here], axis=0, keepdims=True) / gain_own

    scatter_stage(0, 4)
    attend_back(0)
    send_lates(5, 6)
    scatter_stage(1, 1)
    scatter_stage(0, 5)
    attend_back(1)
    send_lates(6, 7)
    scatter_stage(1, 2)
    scatter_stage(0, 6)
    early_grads(0, 2)
    attend_back(2)
    send_lates(7, 16 - EARLY)
    scatter_stage(1, 3)
    early_grads(2, 4)
    attend_back(3)
    top_early(0, EARLY // 2)
    scatter_stage(1, 4)
    top_early(EARLY // 2, EARLY)
    scatter_stage(1, 5)
    early_grads(4, EARLY)
    finish(0)
    scatter_stage(1, 6)

    @pl.when(is_low)
    def _():
        send_inv1.wait_recv()
        send_gain1.wait_recv()
        send_cen1.wait_recv()
        inv1[...] = jnp.broadcast_to(inv1_row[0:1, :], (TOK, 128)).T
        cen1[...] = jnp.broadcast_to(cen1_row[0:1, :], (TOK, 128)).T
        for e in range(EARLY):
            ng1_copies[e].wait_recv()
            early[e][1].wait_recv()
            here = pl.ds(e * 512, 512)
            where = cols(early[e][0] * 512, 512)
            upper = branch(hid1[:, here], inv1, ng1[:, here], gain1[:, where], cen1)
            upper = (top[:, where].astype(F32) + upper).astype(BF16)
            stream[:, where] = (upper.astype(F32) + own[:, where]).astype(BF16)
        for e, (j, copy) in enumerate(lates):
            copy.wait_recv()
            where = cols(j * 512, 512)
            upper = late[:, pl.ds(e * 512, 512)].astype(F32)
            stream[:, where] = (upper + own[:, where]).astype(BF16)

    finish(1)

    for copy, who in sent:
        if who is None:
            copy.wait_send()

    @pl.when(is_top)
    def _():
        for copy, who in sent:
            if who == "down":
                copy.wait_send()

    @pl.when(is_low)
    def _():
        for copy, who in sent:
            if who == "low":
                copy.wait_send()


def store_kernel(*refs):
    parts, outs, sems = refs[:5], refs[5:10], refs[10]
    copies = [pltpu.make_async_copy(parts[n], outs[n], sems.at[n]) for n in range(5)]
    for copy in copies:
        copy.start()
    for copy in copies:
        copy.wait()


def per_device(hidden_in, query_rows, key_rows, context_grad, stream_top, norm_gain, value_weight):
    def vmem(*shape, dtype=BF16):
        return pltpu.VMEM(shape, dtype)

    scratch = [
        vmem(TOK, D), vmem(TOK, D // 2), vmem(TOK, 4096), vmem(TOK, KVW), vmem(TOK, 4096), vmem(TOK, D),
        vmem(1, D, dtype=F32), vmem(1, D, dtype=F32),
        *[vmem(TOK, 128, dtype=F32) for _ in range(5)], *[vmem(8, 128, dtype=F32) for _ in range(4)],
        vmem(16, BLK, KVW), vmem(EARLY, BLK, KVW), vmem(2 * TOK, 4096),
        vmem(2 * TOK, KVW), vmem(2 * TOK, KVW), vmem(KVW, 2 * TOK),
        vmem(KV, TOK, GROUP * TOK, dtype=F32),
        vmem(2 * TOK, KVW, dtype=F32), vmem(TOK, KVW, dtype=F32), vmem(TOK, KVW),
        vmem(TOK, D), vmem(16, TOK, BLK), vmem(TOK, EARLY * 512), vmem(EARLY, TOK, BLK),
        vmem(TOK, EARLY * 512), vmem(TOK, (16 - EARLY) * 512), vmem(TOK, D, dtype=F32),
        vmem(16, KVW, BLK), vmem(20, 6, 128, 128), vmem(2, 4, 128, 128, dtype=F32),
        vmem(2, 4, 128, 128), vmem(2, 3, 128, 128), vmem(2, 4, 128, 128), vmem(KVW, BLK, dtype=F32),
        pltpu.SemaphoreType.DMA((NSEM,)), pltpu.SemaphoreType.DMA((NSEM,)), pltpu.SemaphoreType.DMA((32,)),
    ]
    out_shapes = (((TOK, D), BF16), ((TOK, 4096), BF16), ((TOK, KVW), BF16), ((BLK, KVW), F32), ((1, BLK), F32))
    args = hidden_in[0], query_rows[0], key_rows[0], context_grad[0], stream_top, norm_gain, value_weight[0]
    parts = pl.pallas_call(
        kernel,
        out_shape=tuple(pltpu.VMEM(*shape) for shape in out_shapes),
        in_specs=[pl.BlockSpec(memory_space=pl.ANY)] * 7,
        out_specs=[pl.BlockSpec(memory_space=pltpu.VMEM)] * 5,
        scratch_shapes=scratch,
        compiler_params=pltpu.CompilerParams(
            collective_id=0, has_side_effects=True, vmem_limit_bytes=48 * 1024 * 1024
        ),
        cost_estimate=pl.CostEstimate(flops=5 * 10**9, bytes_accessed=12 * 10**6, transcendentals=10**6),
    )(*[pltpu.with_memory_space_constraint(arg, pltpu.HBM) for arg in args])
    outs = pl.pallas_call(
        store_kernel,
        out_shape=tuple(jax.ShapeDtypeStruct(*shape) for shape in out_shapes),
        in_specs=[pl.BlockSpec(memory_space=pltpu.VMEM)] * 5,
        out_specs=[pl.BlockSpec(memory_space=pl.ANY)] * 5,
        scratch_shapes=[pltpu.SemaphoreType.DMA((5,))],
        compiler_params=pltpu.CompilerParams(vmem_limit_bytes=1024 * 1024),
    )(*[pltpu.with_memory_space_constraint(part, pltpu.VMEM) for part in parts])
    stream, query_grad, key_grad, weight_grad, gain_grad = outs
    return stream[None], query_grad[None], key_grad[None], weight_grad[None], gain_grad


def solution(mesh):
    return jax.shard_map(
        per_device,
        mesh=mesh,
        in_specs=(
            P("pipe", ("rep", "shard"), None),
            P("pipe", ("rep", "shard"), None),
            P("pipe", ("rep", "shard"), None),
            P("pipe", ("rep", "shard"), None),
            P(("rep", "shard"), None),
            P("pipe", None),
            P("pipe", "shard", None),
        ),
        out_specs=(
            P("pipe", ("rep", "shard"), None),
            P("pipe", ("rep", "shard"), None),
            P("pipe", ("rep", "shard"), None),
            P("pipe", "shard", None),
            P("pipe", "shard"),
        ),
        check_vma=False,
    )
```

```python
import itertools

import jax
import jax.numpy as jnp
from jax import lax
from jax.experimental import pallas as pl
from jax.experimental.pallas import tpu as pltpu
from jax.sharding import PartitionSpec as P

D = 8192
HEAD = 128
QHEADS = 32
KV = 4
GROUP = QHEADS // KV
TOK = 128
KVW = KV * HEAD
BLK = 256
EPSILON = 1e-05
SCORE_SCALE = 1.0 / HEAD**0.5
GRAD_SCALE = 16384.0**-0.5
F32, BF16 = jnp.float32, jnp.bfloat16

ORDER = (
    (0, 0), (3, 0), (1, 0), (0, 3), (0, 1), (2, 0), (0, 2),
    (3, 3), (1, 3), (3, 1), (1, 1), (2, 3), (2, 1), (3, 2), (1, 2), (2, 2),
)
EARLY = 8
NSEM = 164 + 3 * EARLY


def dot(a, b):
    return jnp.dot(a, b, preferred_element_type=F32)


def dot_nt(a, b):
    return lax.dot_general(a, b, (((1,), (1,)), ((), ())), preferred_element_type=F32)


def kernel(
    hid_h, query_h, key_h, ctx_h, top_h, gain_h, w_h,
    stream, qg, kg, vwg, gg,
    hid, hsib, query, key, ctx, top, gain, gain1, inv, inv_sib, inv1, cen, cen1,
    inv_row, inv1_row, cen_row, cen1_row,
    w_all, w1, normed, vg, vg1, vgt, probs, vpart, vrecv, values,
    ng, ng_stage, ng1, ng1_stage, hid1, late, own,
    wt, rfirst, rlast, fin, rep_stage, rep_recv, rep_all, wown,
    ssem, rsem, lsem,
):
    pipe = lax.axis_index("pipe")
    rep = lax.axis_index("rep")
    shard = lax.axis_index("shard")
    core = lax.rem(shard, 2)
    chip = lax.div(shard, 2)
    x, y = lax.rem(chip, 4), lax.div(chip, 4)
    is_top = pipe == 1
    is_low = pipe == 0
    ids = itertools.count()
    local_ids = itertools.count()
    sent = []

    def chip_at(dx, dy):
        return lax.rem(y + dy % 4, 4) * 4 + lax.rem(x + dx % 4, 4)

    def peer(dx, dy):
        return {"shard": chip_at(dx, dy) * 2 + core}

    sibling = {"shard": chip * 2 + (1 - core)}
    below = {"pipe": 0}
    ahead = {"pipe": 0, "rep": lax.rem(rep + 1, 4)}

    def remote(src, dst, device, who=None):
        number = next(ids)
        copy = pltpu.make_async_remote_copy(
            src_ref=src, dst_ref=dst, send_sem=ssem.at[number], recv_sem=rsem.at[number],
            device_id=device, device_id_type=pl.DeviceIdType.MESH,
        )
        sent.append((copy, who))
        return copy

    def send(src, dst, device):
        copy = remote(src, dst, device)
        copy.start()
        return copy

    def local(src, dst):
        copy = pltpu.make_async_copy(src, dst, lsem.at[next(local_ids)])
        copy.start()
        return copy

    def cols(start, width):
        return pl.ds(pl.multiple_of(start, 128), width)

    barrier = pltpu.get_barrier_semaphore()
    partners = [peer(1, 0), peer(3, 0), peer(0, 1), peer(0, 3), sibling, {"pipe": 1 - pipe}]
    partners += [{"rep": lax.rem(rep + o, 4)} for o in (1, 3)]
    partners += [{"pipe": 1 - pipe, "rep": lax.rem(rep + jnp.where(is_top, 1, 3), 4)}]
    for device in partners:
        pl.semaphore_signal(barrier, inc=1, device_id=device, device_id_type=pl.DeviceIdType.MESH)
    load_hid = local(hid_h, hid)
    load_gain = local(gain_h, gain)
    load_key = local(key_h, key)
    load_query = local(query_h, query)
    load_ctx = local(ctx_h, ctx)
    load_w = local(w_h, w_all.at[chip])
    load_top = local(top_h, top)

    pl.semaphore_wait(barrier, len(partners))

    def step(half, first, by):
        along_x = (half == 0) == first
        return (by, 0) if along_x else (0, by)

    def shift(half, first_by, second_by):
        return (first_by, second_by) if half == 0 else (second_by, first_by)

    def rows(half, quarter=None):
        if quarter is None:
            return pl.ds(half * 128, 128)
        return pl.ds(half * 128 + quarter * 64, 64)

    gather = {}

    def gather_own(half, first):
        for kind, by in ((0, 1), (1, 3)):
            src = w_h.at[rows(half), :]
            gather[half, first, 0, kind] = send(
                src, w_all.at[chip, rows(half), :], peer(*step(half, first, by))
            )

    def gather_pass(half, offset, index):
        j = chip_at(*shift(half, offset, 0))
        for kind, by in ((0, 1), (1, 3)):
            part = w_all.at[j, rows(half), :]
            gather[half, False, index, kind] = send(part, part, peer(*step(half, False, by)))

    def gather_forward(half, first, index, offset):
        for kind, by in ((0, 3), (1, 1)):
            gather[half, first, index, kind].wait_recv()
            move = shift(half, by, 0) if first else shift(half, offset, by)
            part = w_all.at[chip_at(*move), rows(half, kind), :]
            to = 1 if kind == 0 else 3
            gather[half, first, index, kind + 2] = send(part, part, peer(*step(half, first, to)))

    def gather_end(half, first, index):
        for kind in (2, 3):
            gather[half, first, index, kind].wait_recv()

    early = []
    for e in range(EARLY):
        j = chip_at(*ORDER[e])
        early.append((
            j,
            remote(hid_h.at[:, cols(j * 512, 512)], hid1.at[:, pl.ds(e * 512, 512)], below, "down"),
            [
                remote((w_h if e == 0 else w_all.at[j]).at[rows(half), :], w1.at[e, rows(half), :], ahead, "down")
                for half in (0, 1)
            ],
        ))
    send_gain1 = remote(gain_h, gain1, below, "down")

    for half in (0, 1):
        gather_own(half, True)
    for half in (0, 1):
        gather_own(half, False)
    hsib_copies = []
    for j in range(16):
        hsib_copies.append(send(
            hid_h.at[:, cols((2 * j + 1 - core) * BLK, BLK)], hsib.at[:, pl.ds(j * BLK, BLK)], sibling
        ))

    @pl.when(is_top)
    def _():
        early[0][2][0].start()
        early[0][2][1].start()
        send_gain1.start()
        for _, down, _ in early:
            down.start()

    load_hid.wait()
    load_gain.wait()

    def square(i, total):
        part = hid[:, cols(i * 512, 512)].astype(F32)
        part = part * part
        for n in range(4):
            total = total + part[:, n * 128:(n + 1) * 128]
        return total

    total = lax.fori_loop(0, 16, square, jnp.zeros((TOK, 128), F32))
    mean = jnp.sum(total, axis=1, keepdims=True) * (1.0 / D)
    inv[...] = jnp.broadcast_to(lax.rsqrt(mean + EPSILON), (TOK, 128))
    send_inv = send(inv, inv_sib, sibling)
    inv_row[...] = inv[...].T[0:8, :]
    send_inv1 = remote(inv_row, inv1_row, below, "down")

    @pl.when(is_top)
    def _():
        send_inv1.start()

    load_key.wait()
    load_query.wait()
    load_ctx.wait()

    def stacked(ref, k):
        return jnp.concatenate(
            [ref[:, (GROUP * k + g) * HEAD:(GROUP * k + g + 1) * HEAD] for g in range(GROUP)], axis=0
        )

    def attend(k):
        lanes = slice(k * HEAD, (k + 1) * HEAD)
        scores = dot_nt(key[:, lanes], stacked(query, k)) * SCORE_SCALE
        u = lax.broadcasted_iota(jnp.int32, scores.shape, 0)
        t = lax.broadcasted_iota(jnp.int32, scores.shape, 1) & (TOK - 1)
        scores = jnp.where(u <= t, scores, -1e30)
        raw = jnp.exp(scores - jnp.max(scores, axis=0, keepdims=True))
        prob = raw / jnp.sum(raw, axis=0, keepdims=True)
        probs[k] = prob
        vg[0:TOK, lanes] = dot(prob.astype(BF16), stacked(ctx, k)).astype(BF16)

    def top_blocks_ahead(pairs):
        @pl.when(is_top)
        def _():
            for e, half in pairs:
                early[e][2][half].start()

    attend(0)
    attend(1)
    for half in (0, 1):
        gather_forward(half, True, 0, 0)
        gather_pass(half, 3, 1)
        gather_pass(half, 1, 2)
    top_blocks_ahead(((1, 0), (2, 0), (3, 1), (4, 1)))
    attend(2)
    attend(3)

    send_vg = send(vg.at[pl.ds(0, TOK), :], vg.at[pl.ds(TOK, TOK), :], sibling)
    send_vg1 = remote(vg.at[pl.ds(0, TOK), :], vg1.at[pl.ds(0, TOK), :], below, "down")

    @pl.when(is_top)
    def _():
        send_vg1.start()

    for half in (0, 1):
        gather_forward(half, False, 0, 0)
    load_w.wait()
    top_blocks_ahead(((1, 1), (2, 1), (3, 0), (4, 0)))

    for copy in hsib_copies:
        copy.wait_recv()
    send_inv.wait_recv()

    def norm_block(j, carry):
        gain_row = gain[:, cols((2 * j + core) * BLK, BLK)]
        mine = hid[:, cols((2 * j + core) * BLK, BLK)].astype(F32) * inv[:, 0:1]
        other = hsib[:, cols(j * BLK, BLK)].astype(F32) * inv_sib[:, 0:1]
        normed[0:TOK, cols(j * BLK, BLK)] = (mine * gain_row).astype(BF16)
        normed[TOK:, cols(j * BLK, BLK)] = (other * gain_row).astype(BF16)
        return carry

    lax.fori_loop(0, 16, norm_block, 0)
    for half in (0, 1):
        gather_end(half, True, 0)
        gather_pass(half, 2, 3)

    send_vg.wait_recv()
    vgt[...] = vg[...].astype(F32).T.astype(BF16)

    def weight_block(place, carry):
        dx, dy = lax.div(place, 4), lax.rem(place, 4)
        j = lax.rem(y + dy, 4) * 4 + lax.rem(x + dx, 4)
        wt[dx, dy] = dot(vgt[...], normed[:, cols(j * BLK, BLK)]).astype(BF16)
        return carry

    lax.fori_loop(0, 8, weight_block, 0)
    for half in (0, 1):
        gather_end(half, False, 0)
    top_blocks_ahead(((5, 0), (5, 1), (6, 0), (6, 1)))
    for half in (0, 1):
        gather_forward(half, False, 1, 3)
        gather_forward(half, False, 2, 1)
    top_blocks_ahead(tuple((e, half) for e in range(7, EARLY) for half in (0, 1)))
    lax.fori_loop(8, 16, weight_block, 0)

    def value_block(place):
        j = chip_at(*ORDER[place])
        part = dot(normed[:, cols(j * BLK, BLK)], w_all[j])
        if place == 0:
            vpart[...] = part
        else:
            vpart[...] += part

    ng_copies = {}
    ng_waited = set()

    def grad_block(place):
        j = chip_at(*ORDER[place])
        grad = dot_nt(vg[...], w_all[j])
        where = cols((2 * j + core) * BLK, BLK)
        ng[:, where] = grad[0:TOK].astype(BF16)
        ng_stage[place] = grad[TOK:].astype(BF16)
        ng_copies[place] = send(ng_stage.at[place], ng.at[:, where], sibling)

    def grads_ready(start, stop):
        for place in range(start, stop):
            if place not in ng_waited:
                ng_waited.add(place)
                ng_copies[place].wait_recv()

    def wrows(half, quarter):
        return pl.ds(half * 256 + quarter * 128, 128)

    scatter = {}

    def lanes_of(wave):
        return pl.ds(wave * 128, 128)

    def term(wave, half, first, by, quarter):
        along, across = (by, slice(None)) if first else (0, by)
        place = (along, across) if half == 0 else (across, along)
        return wt.at[place[0], place[1], wrows(half, quarter), lanes_of(wave)]

    def landing(wave, half, first, kind):
        return (rfirst if first else rlast).at[wave, half, kind]

    def scatter_make(wave, half, first, kind, by, quarter, to):
        scatter[wave, half, first, kind] = remote(
            term(wave, half, first, by, quarter),
            landing(wave, half, first, kind),
            peer(*step(half, first, to)),
        )
        return scatter[wave, half, first, kind]

    def scatter_open(wave, first):
        copies = []
        for kind, by, quarter, to in ((0, 2, 0, 1), (1, 2, 1, 3), (2, 1, 1, 1), (3, 3, 0, 3)):
            for half in (0, 1):
                copies.append(scatter_make(wave, half, first, kind, by, quarter, to))
        return copies

    def add_in(wave, half, first, by, quarter, kinds):
        total = term(wave, half, first, by, quarter)[...].astype(F32)
        for kind in kinds:
            total = total + landing(wave, half, first, kind)[...].astype(F32)
        return total

    def scatter_forward(wave, first):
        for half in (0, 1):
            for kind, by, quarter in ((0, 1, 0), (1, 3, 1)):
                scatter[wave, half, first, kind].wait_recv()
                total = add_in(wave, half, first, by, quarter, (kind,))
                term(wave, half, first, by, quarter)[...] = total.astype(BF16)
                scatter_make(wave, half, first, kind + 4, by, quarter, by).start()

    def scatter_own(wave, first):
        for half in (0, 1):
            for kind in (2, 3, 4, 5):
                scatter[wave, half, first, kind].wait_recv()
            for quarter, kinds in ((0, (3, 4)), (1, (2, 5))):
                total = add_in(wave, half, first, 0, quarter, kinds)
                if first:
                    term(wave, half, first, 0, quarter)[...] = total.astype(BF16)
                else:
                    fin[wave, half * 2 + quarter] = total

    after, before, across = lax.rem(rep + 1, 4), lax.rem(rep + 3, 4), lax.rem(rep + 2, 4)
    halves = (slice(0, 64), slice(64, 128))
    rep_copies = {}

    def rep_send(wave, kind, value, to):
        rep_stage[wave, kind] = value.astype(BF16)
        rep_copies[wave, kind] = send(rep_stage.at[wave, kind], rep_recv.at[wave, kind], {"rep": to})

    def rep_got(wave, kind):
        rep_copies[wave, kind].wait_recv()
        return rep_recv[wave, kind].astype(F32)

    def rep_stage_of(wave, stage):
        if stage == 0:
            rep_send(wave, 0, fin[wave, across, halves[0], :], after)
            rep_send(wave, 1, fin[wave, across, halves[1], :], before)
            rep_send(wave, 2, fin[wave, after, halves[1], :], after)
            rep_send(wave, 3, fin[wave, before, halves[0], :], before)
        elif stage == 1:
            rep_send(wave, 4, fin[wave, after, halves[0], :] + rep_got(wave, 0), after)
            rep_send(wave, 5, fin[wave, before, halves[1], :] + rep_got(wave, 1), before)
        elif stage == 2:
            for half, kinds in ((0, (3, 4)), (1, (2, 5))):
                total = fin[wave, rep, halves[half], :]
                for kind in kinds:
                    total = total + rep_got(wave, kind)
                rep_all[wave, rep, halves[half], :] = total.astype(BF16)
            for kind, to in ((6, after), (7, before)):
                here = rep_all.at[wave, rep]
                rep_copies[wave, kind] = send(here, here, {"rep": to})
        elif stage == 3:
            for kind, part, half, to in ((6, before, 0, after), (7, after, 1, before)):
                rep_copies[wave, kind].wait_recv()
                here = rep_all.at[wave, part, pl.ds(64 * half, 64), :]
                rep_copies[wave, kind + 2] = send(here, here, {"rep": to})
        else:
            for kind in (8, 9):
                rep_copies[wave, kind].wait_recv()

    def scatter_stage(wave, stage):
        if stage == 0:
            scatter_forward(wave, True)
        elif stage == 1:
            scatter_own(wave, True)
            for copy in scatter_open(wave, False):
                copy.start()
        elif stage == 2:
            scatter_forward(wave, False)
        elif stage == 3:
            scatter_own(wave, False)
            rep_stage_of(wave, 0)

    opening = scatter_open(0, True) + scatter_open(1, True)

    def open_scatter():
        for copy in opening:
            copy.start()

    for place in range(0, 7):
        value_block(place)
    for half in (0, 1):
        gather_forward(half, False, 3, 2)
    for place in range(7, 11):
        value_block(place)
    for half in (0, 1):
        gather_end(half, False, 1)
        gather_end(half, False, 2)
    for place in range(11, 15):
        value_block(place)
    for half in (0, 1):
        gather_end(half, False, 3)
    open_scatter()
    value_block(15)
    send_part = send(vpart.at[pl.ds(TOK, TOK), :], vrecv, sibling)
    for place in range(EARLY, EARLY + 4):
        grad_block(place)

    send_part.wait_recv()
    whole = vpart[0:TOK, :] + vrecv[...]
    values[...] = whole.astype(BF16)
    mean = jnp.sum(whole * vg[0:TOK, :].astype(F32), axis=1, keepdims=True) * (1.0 / D)
    cen[...] = jnp.broadcast_to(mean, (TOK, 128))
    cen_row[...] = cen[...].T[0:8, :]
    send_cen1 = remote(cen_row, cen1_row, below, "down")

    load_top.wait()

    def branch(hidden, scale, grad, gain_row, center):
        factor = scale[:, 0:1]
        normalized = hidden.astype(F32) * factor
        return factor * (grad.astype(F32) * gain_row - normalized * center[:, 0:1])

    def own_branch(where):
        return branch(hid[:, where], inv, ng[:, where], gain[:, where], cen)

    lates = []
    for e in range(EARLY, 16):
        j = chip_at(*ORDER[e])
        where = cols(j * 512, 512)
        lates.append((j, remote(
            stream.at[:, where], late.at[:, pl.ds((e - EARLY) * 512, 512)], below, "down"
        )))
    def top_block(j):
        where = cols(j * 512, 512)
        stream[:, where] = (top[:, where].astype(F32) + own_branch(where)).astype(BF16)

    def own_blocks(start, stop):
        @pl.when(is_low)
        def _():
            for place in range(start, stop):
                where = cols(chip_at(*ORDER[place]) * 512, 512)
                own[:, where] = own_branch(where)

    def send_lates(start, stop):
        grads_ready(EARLY + start, EARLY + stop)
        own_blocks(EARLY + start, EARLY + stop)

        @pl.when(is_top)
        def _():
            if start == 0:
                send_cen1.start()
            for j, copy in lates[start:stop]:
                top_block(j)
                copy.start()

    def top_early(start, stop):
        grads_ready(start, stop)
        own_blocks(start, stop)

        @pl.when(is_top)
        def _():
            for j, _, _ in early[start:stop]:
                top_block(j)

    send_lates(0, 2)
    scatter_stage(0, 0)
    for place in range(EARLY + 4, 16):
        grad_block(place)
    send_lates(2, 4)
    scatter_stage(1, 0)
    send_lates(4, 6)
    for place in range(0, EARLY):
        grad_block(place)
    scatter_stage(0, 1)
    send_lates(6, 16 - EARLY)

    def attend_back(k):
        lanes = slice(k * HEAD, (k + 1) * HEAD)
        queries, grads = stacked(query, k), stacked(ctx, k)
        prob = probs[k]
        grad_prob = dot_nt(values[:, lanes], grads)
        row_dot = jnp.sum(prob * grad_prob, axis=0, keepdims=True)
        wide = prob * (grad_prob - row_dot) * SCORE_SCALE
        grad_score = wide.astype(BF16)
        kg[:, lanes] = dot(grad_score, queries).astype(BF16)
        for g in range(GROUP):
            turned = wide[:, g * HEAD:(g + 1) * HEAD].T.astype(BF16)
            head = (GROUP * k + g) * HEAD
            qg[:, head:head + HEAD] = dot(turned, key[:, lanes]).astype(BF16)

    ng1_copies = []
    forward_vg1 = remote(vg1.at[pl.ds(0, TOK), :], vg1.at[pl.ds(TOK, TOK), :], sibling, "low")
    for e in range(EARLY):
        where = cols(e * 512 + core * BLK, BLK)
        ng1_copies.append(remote(ng1_stage.at[e], ng1.at[:, where], sibling, "low"))

    @pl.when(is_low)
    def _():
        send_vg1.wait_recv()
        forward_vg1.start()

    def early_grads(start, stop):
        @pl.when(is_low)
        def _():
            if start == 0:
                forward_vg1.wait_recv()
            for e in range(start, stop):
                for half in (0, 1):
                    early[e][2][half].wait_recv()
                grad = dot_nt(vg1[...], w1[e])
                ng1[:, cols(e * 512 + core * BLK, BLK)] = grad[0:TOK].astype(BF16)
                ng1_stage[e] = grad[TOK:].astype(BF16)
                ng1_copies[e].start()

    wown[...] = w_all[chip].astype(F32).T

    def finish(wave):
        rep_stage_of(wave, 4)
        summed = jnp.concatenate([rep_all[wave, q].astype(F32) for q in range(4)], axis=0) * GRAD_SCALE
        here = slice(wave * 128, wave * 128 + 128)
        vwg[here, :] = summed.T
        gain_own = gain[:, cols(shard * BLK + wave * 128, 128)]
        gg[:, here] = jnp.sum(summed * wown[:, here], axis=0, keepdims=True) / gain_own

    scatter_stage(0, 2)
    attend_back(0)
    scatter_stage(1, 1)
    scatter_stage(0, 3)
    scatter_stage(1, 2)
    attend_back(1)
    rep_stage_of(0, 1)
    scatter_stage(1, 3)
    attend_back(2)
    rep_stage_of(0, 2)
    rep_stage_of(1, 1)
    attend_back(3)
    early_grads(0, 2)
    rep_stage_of(0, 3)
    rep_stage_of(1, 2)
    early_grads(2, EARLY)
    top_early(0, 4)
    rep_stage_of(1, 3)
    top_early(4, EARLY)
    finish(0)

    @pl.when(is_low)
    def _():
        send_inv1.wait_recv()
        send_gain1.wait_recv()
        send_cen1.wait_recv()
        inv1[...] = jnp.broadcast_to(inv1_row[0:1, :], (TOK, 128)).T
        cen1[...] = jnp.broadcast_to(cen1_row[0:1, :], (TOK, 128)).T
        for e in range(EARLY):
            ng1_copies[e].wait_recv()
            early[e][1].wait_recv()
            here = pl.ds(e * 512, 512)
            where = cols(early[e][0] * 512, 512)
            upper = branch(hid1[:, here], inv1, ng1[:, here], gain1[:, where], cen1)
            upper = (top[:, where].astype(F32) + upper).astype(BF16)
            stream[:, where] = (upper.astype(F32) + own[:, where]).astype(BF16)
        for e, (j, copy) in enumerate(lates):
            copy.wait_recv()
            where = cols(j * 512, 512)
            upper = late[:, pl.ds(e * 512, 512)].astype(F32)
            stream[:, where] = (upper + own[:, where]).astype(BF16)

    finish(1)

    for copy, who in sent:
        if who is None:
            copy.wait_send()

    @pl.when(is_top)
    def _():
        for copy, who in sent:
            if who == "down":
                copy.wait_send()

    @pl.when(is_low)
    def _():
        for copy, who in sent:
            if who == "low":
                copy.wait_send()


def store_kernel(*refs):
    parts, outs, sems = refs[:5], refs[5:10], refs[10]
    copies = [pltpu.make_async_copy(parts[n], outs[n], sems.at[n]) for n in range(5)]
    for copy in copies:
        copy.start()
    for copy in copies:
        copy.wait()


def per_device(hidden_in, query_rows, key_rows, context_grad, stream_top, norm_gain, value_weight):
    def vmem(*shape, dtype=BF16):
        return pltpu.VMEM(shape, dtype)

    scratch = [
        vmem(TOK, D), vmem(TOK, D // 2), vmem(TOK, 4096), vmem(TOK, KVW), vmem(TOK, 4096), vmem(TOK, D),
        vmem(1, D, dtype=F32), vmem(1, D, dtype=F32),
        *[vmem(TOK, 128, dtype=F32) for _ in range(5)], *[vmem(8, 128, dtype=F32) for _ in range(4)],
        vmem(16, BLK, KVW), vmem(EARLY, BLK, KVW), vmem(2 * TOK, 4096),
        vmem(2 * TOK, KVW), vmem(2 * TOK, KVW), vmem(KVW, 2 * TOK),
        vmem(KV, TOK, GROUP * TOK, dtype=F32),
        vmem(2 * TOK, KVW, dtype=F32), vmem(TOK, KVW, dtype=F32), vmem(TOK, KVW),
        vmem(TOK, D), vmem(16, TOK, BLK), vmem(TOK, EARLY * 512), vmem(EARLY, TOK, BLK),
        vmem(TOK, EARLY * 512), vmem(TOK, (16 - EARLY) * 512), vmem(TOK, D, dtype=F32),
        vmem(4, 4, KVW, BLK), vmem(2, 2, 6, 4, 128, 128), vmem(2, 2, 6, 128, 128), vmem(2, 4, 128, 128, dtype=F32),
        vmem(2, 6, 64, 128), vmem(2, 6, 64, 128), vmem(2, 4, 128, 128), vmem(KVW, BLK, dtype=F32),
        pltpu.SemaphoreType.DMA((NSEM,)), pltpu.SemaphoreType.DMA((NSEM,)), pltpu.SemaphoreType.DMA((32,)),
    ]
    out_shapes = (((TOK, D), BF16), ((TOK, 4096), BF16), ((TOK, KVW), BF16), ((BLK, KVW), F32), ((1, BLK), F32))
    args = hidden_in[0], query_rows[0], key_rows[0], context_grad[0], stream_top, norm_gain, value_weight[0]
    parts = pl.pallas_call(
        kernel,
        out_shape=tuple(pltpu.VMEM(*shape) for shape in out_shapes),
        in_specs=[pl.BlockSpec(memory_space=pl.ANY)] * 7,
        out_specs=[pl.BlockSpec(memory_space=pltpu.VMEM)] * 5,
        scratch_shapes=scratch,
        compiler_params=pltpu.CompilerParams(
            collective_id=0, has_side_effects=True, vmem_limit_bytes=48 * 1024 * 1024
        ),
        cost_estimate=pl.CostEstimate(flops=5 * 10**9, bytes_accessed=12 * 10**6, transcendentals=10**6),
    )(*[pltpu.with_memory_space_constraint(arg, pltpu.HBM) for arg in args])
    outs = pl.pallas_call(
        store_kernel,
        out_shape=tuple(jax.ShapeDtypeStruct(*shape) for shape in out_shapes),
        in_specs=[pl.BlockSpec(memory_space=pltpu.VMEM)] * 5,
        out_specs=[pl.BlockSpec(memory_space=pl.ANY)] * 5,
        scratch_shapes=[pltpu.SemaphoreType.DMA((5,))],
        compiler_params=pltpu.CompilerParams(vmem_limit_bytes=1024 * 1024),
    )(*[pltpu.with_memory_space_constraint(part, pltpu.VMEM) for part in parts])
    stream, query_grad, key_grad, weight_grad, gain_grad = outs
    return stream[None], query_grad[None], key_grad[None], weight_grad[None], gain_grad


def solution(mesh):
    return jax.shard_map(
        per_device,
        mesh=mesh,
        in_specs=(
            P("pipe", ("rep", "shard"), None),
            P("pipe", ("rep", "shard"), None),
            P("pipe", ("rep", "shard"), None),
            P("pipe", ("rep", "shard"), None),
            P(("rep", "shard"), None),
            P("pipe", None),
            P("pipe", "shard", None),
        ),
        out_specs=(
            P("pipe", ("rep", "shard"), None),
            P("pipe", ("rep", "shard"), None),
            P("pipe", ("rep", "shard"), None),
            P("pipe", "shard", None),
            P("pipe", "shard"),
        ),
        check_vma=False,
    )
```

```python
import itertools

import jax
import jax.numpy as jnp
from jax import lax
from jax.experimental import pallas as pl
from jax.experimental.pallas import tpu as pltpu
from jax.sharding import PartitionSpec as P

D = 8192
HEAD = 128
QHEADS = 32
KV = 4
GROUP = QHEADS // KV
TOK = 128
KVW = KV * HEAD
BLK = 256
EPSILON = 1e-05
SCORE_SCALE = 1.0 / HEAD**0.5
GRAD_SCALE = 16384.0**-0.5
F32, BF16 = jnp.float32, jnp.bfloat16

ORDER = (
    (0, 0), (3, 0), (1, 0), (0, 3), (0, 1), (2, 0), (0, 2),
    (3, 3), (1, 3), (3, 1), (1, 1), (2, 3), (2, 1), (3, 2), (1, 2), (2, 2),
)
EARLY = 8
NSEM = 164 + 3 * EARLY


def dot(a, b):
    return jnp.dot(a, b, preferred_element_type=F32)


def dot_nt(a, b):
    return lax.dot_general(a, b, (((1,), (1,)), ((), ())), preferred_element_type=F32)


def kernel(
    hid_h, query_h, key_h, ctx_h, top_h, gain_h, w_h,
    stream, qg, kg, vwg, gg,
    hid, hsib, query, key, ctx, top, gain, gain1, inv, inv_sib, inv1, cen, cen1,
    inv_row, inv1_row, cen_row, cen1_row,
    w_all, w1, normed, vg, vg1, vgt, probs, vpart, vrecv, values,
    ng, ng_stage, ng1, ng1_stage, hid1, late, own,
    wt, rfirst, rlast, fin, rep_stage, rep_recv, rep_all, wown,
    ssem, rsem, lsem,
):
    pipe = lax.axis_index("pipe")
    rep = lax.axis_index("rep")
    shard = lax.axis_index("shard")
    core = lax.rem(shard, 2)
    chip = lax.div(shard, 2)
    x, y = lax.rem(chip, 4), lax.div(chip, 4)
    is_top = pipe == 1
    is_low = pipe == 0
    ids = itertools.count()
    local_ids = itertools.count()
    sent = []

    def chip_at(dx, dy):
        return lax.rem(y + dy % 4, 4) * 4 + lax.rem(x + dx % 4, 4)

    def peer(dx, dy):
        return {"shard": chip_at(dx, dy) * 2 + core}

    sibling = {"shard": chip * 2 + (1 - core)}
    below = {"pipe": 0}
    ahead = {"pipe": 0, "rep": lax.rem(rep + 1, 4)}

    def remote(src, dst, device, who=None):
        number = next(ids)
        copy = pltpu.make_async_remote_copy(
            src_ref=src, dst_ref=dst, send_sem=ssem.at[number], recv_sem=rsem.at[number],
            device_id=device, device_id_type=pl.DeviceIdType.MESH,
        )
        sent.append((copy, who))
        return copy

    def send(src, dst, device):
        copy = remote(src, dst, device)
        copy.start()
        return copy

    def local(src, dst):
        copy = pltpu.make_async_copy(src, dst, lsem.at[next(local_ids)])
        copy.start()
        return copy

    def cols(start, width):
        return pl.ds(pl.multiple_of(start, 128), width)

    barrier = pltpu.get_barrier_semaphore()
    partners = [peer(1, 0), peer(3, 0), peer(0, 1), peer(0, 3), sibling, {"pipe": 1 - pipe}]
    partners += [{"rep": lax.rem(rep + o, 4)} for o in (1, 3)]
    partners += [{"pipe": 1 - pipe, "rep": lax.rem(rep + jnp.where(is_top, 1, 3), 4)}]
    for device in partners:
        pl.semaphore_signal(barrier, inc=1, device_id=device, device_id_type=pl.DeviceIdType.MESH)
    load_hid = local(hid_h, hid)
    load_gain = local(gain_h, gain)
    load_key = local(key_h, key)
    load_query = local(query_h, query)
    load_ctx = local(ctx_h, ctx)
    load_w = local(w_h, w_all.at[chip])
    load_top = local(top_h, top)

    pl.semaphore_wait(barrier, len(partners))

    def step(half, first, by):
        along_x = (half == 0) == first
        return (by, 0) if along_x else (0, by)

    def shift(half, first_by, second_by):
        return (first_by, second_by) if half == 0 else (second_by, first_by)

    def rows(half, quarter=None):
        if quarter is None:
            return pl.ds(half * 128, 128)
        return pl.ds(half * 128 + quarter * 64, 64)

    gather = {}

    def gather_own(half, first):
        for kind, by in ((0, 1), (1, 3)):
            src = w_h.at[rows(half), :]
            gather[half, first, 0, kind] = send(
                src, w_all.at[chip, rows(half), :], peer(*step(half, first, by))
            )

    def gather_pass(half, offset, index):
        j = chip_at(*shift(half, offset, 0))
        for kind, by in ((0, 1), (1, 3)):
            part = w_all.at[j, rows(half), :]
            gather[half, False, index, kind] = send(part, part, peer(*step(half, False, by)))

    def gather_forward(half, first, index, offset):
        for kind, by in ((0, 3), (1, 1)):
            gather[half, first, index, kind].wait_recv()
            move = shift(half, by, 0) if first else shift(half, offset, by)
            part = w_all.at[chip_at(*move), rows(half, kind), :]
            to = 1 if kind == 0 else 3
            gather[half, first, index, kind + 2] = send(part, part, peer(*step(half, first, to)))

    def gather_end(half, first, index):
        for kind in (2, 3):
            gather[half, first, index, kind].wait_recv()

    early = []
    for e in range(EARLY):
        j = chip_at(*ORDER[e])
        early.append((
            j,
            remote(hid_h.at[:, cols(j * 512, 512)], hid1.at[:, pl.ds(e * 512, 512)], below, "down"),
            [
                remote((w_h if e == 0 else w_all.at[j]).at[rows(half), :], w1.at[e, rows(half), :], ahead, "down")
                for half in (0, 1)
            ],
        ))
    send_gain1 = remote(gain_h, gain1, below, "down")

    for half in (0, 1):
        gather_own(half, True)
    for half in (0, 1):
        gather_own(half, False)
    hsib_copies = []
    for j in range(16):
        hsib_copies.append(send(
            hid_h.at[:, cols((2 * j + 1 - core) * BLK, BLK)], hsib.at[:, pl.ds(j * BLK, BLK)], sibling
        ))

    @pl.when(is_top)
    def _():
        early[0][2][0].start()
        early[0][2][1].start()
        send_gain1.start()
        for _, down, _ in early:
            down.start()

    load_hid.wait()
    load_gain.wait()

    def square(i, total):
        part = hid[:, cols(i * 512, 512)].astype(F32)
        part = part * part
        for n in range(4):
            total = total + part[:, n * 128:(n + 1) * 128]
        return total

    total = lax.fori_loop(0, 16, square, jnp.zeros((TOK, 128), F32))
    mean = jnp.sum(total, axis=1, keepdims=True) * (1.0 / D)
    inv[...] = jnp.broadcast_to(lax.rsqrt(mean + EPSILON), (TOK, 128))
    send_inv = send(inv, inv_sib, sibling)
    inv_row[...] = inv[...].T[0:8, :]
    send_inv1 = remote(inv_row, inv1_row, below, "down")

    @pl.when(is_top)
    def _():
        send_inv1.start()

    load_key.wait()
    load_query.wait()
    load_ctx.wait()

    def stacked(ref, k):
        return jnp.concatenate(
            [ref[:, (GROUP * k + g) * HEAD:(GROUP * k + g + 1) * HEAD] for g in range(GROUP)], axis=0
        )

    def attend(k):
        lanes = slice(k * HEAD, (k + 1) * HEAD)
        scores = dot_nt(key[:, lanes], stacked(query, k)) * SCORE_SCALE
        u = lax.broadcasted_iota(jnp.int32, scores.shape, 0)
        t = lax.broadcasted_iota(jnp.int32, scores.shape, 1) & (TOK - 1)
        scores = jnp.where(u <= t, scores, -1e30)
        raw = jnp.exp(scores - jnp.max(scores, axis=0, keepdims=True))
        prob = raw / jnp.sum(raw, axis=0, keepdims=True)
        probs[k] = prob
        vg[0:TOK, lanes] = dot(prob.astype(BF16), stacked(ctx, k)).astype(BF16)

    def top_blocks_ahead(pairs):
        @pl.when(is_top)
        def _():
            for e, half in pairs:
                early[e][2][half].start()

    attend(0)
    attend(1)
    for half in (0, 1):
        gather_forward(half, True, 0, 0)
        gather_pass(half, 3, 1)
        gather_pass(half, 1, 2)
    top_blocks_ahead(((1, 0), (2, 0), (3, 1), (4, 1)))
    attend(2)
    attend(3)

    send_vg = send(vg.at[pl.ds(0, TOK), :], vg.at[pl.ds(TOK, TOK), :], sibling)
    send_vg1 = remote(vg.at[pl.ds(0, TOK), :], vg1.at[pl.ds(0, TOK), :], below, "down")

    @pl.when(is_top)
    def _():
        send_vg1.start()

    for half in (0, 1):
        gather_forward(half, False, 0, 0)
    load_w.wait()
    top_blocks_ahead(((1, 1), (2, 1), (3, 0), (4, 0)))

    for copy in hsib_copies:
        copy.wait_recv()
    send_inv.wait_recv()

    def norm_block(j, carry):
        gain_row = gain[:, cols((2 * j + core) * BLK, BLK)]
        mine = hid[:, cols((2 * j + core) * BLK, BLK)].astype(F32) * inv[:, 0:1]
        other = hsib[:, cols(j * BLK, BLK)].astype(F32) * inv_sib[:, 0:1]
        normed[0:TOK, cols(j * BLK, BLK)] = (mine * gain_row).astype(BF16)
        normed[TOK:, cols(j * BLK, BLK)] = (other * gain_row).astype(BF16)
        return carry

    lax.fori_loop(0, 16, norm_block, 0)
    for half in (0, 1):
        gather_end(half, True, 0)
        gather_pass(half, 2, 3)

    send_vg.wait_recv()
    vgt[...] = vg[...].astype(F32).T.astype(BF16)

    def weight_block(place, carry):
        dx, dy = lax.div(place, 4), lax.rem(place, 4)
        j = lax.rem(y + dy, 4) * 4 + lax.rem(x + dx, 4)
        wt[dx, dy] = dot(vgt[...], normed[:, cols(j * BLK, BLK)]).astype(BF16)
        return carry

    lax.fori_loop(0, 8, weight_block, 0)
    for half in (0, 1):
        gather_end(half, False, 0)
    top_blocks_ahead(((5, 0), (5, 1), (6, 0), (6, 1)))
    for half in (0, 1):
        gather_forward(half, False, 1, 3)
        gather_forward(half, False, 2, 1)
    top_blocks_ahead(tuple((e, half) for e in range(7, EARLY) for half in (0, 1)))
    lax.fori_loop(8, 16, weight_block, 0)

    def value_block(place):
        j = chip_at(*ORDER[place])
        part = dot(normed[:, cols(j * BLK, BLK)], w_all[j])
        if place == 0:
            vpart[...] = part
        else:
            vpart[...] += part

    ng_copies = {}
    ng_waited = set()

    def grad_block(place):
        j = chip_at(*ORDER[place])
        grad = dot_nt(vg[...], w_all[j])
        where = cols((2 * j + core) * BLK, BLK)
        ng[:, where] = grad[0:TOK].astype(BF16)
        ng_stage[place] = grad[TOK:].astype(BF16)
        ng_copies[place] = send(ng_stage.at[place], ng.at[:, where], sibling)

    def grads_ready(start, stop):
        for place in range(start, stop):
            if place not in ng_waited:
                ng_waited.add(place)
                ng_copies[place].wait_recv()

    def wrows(half, quarter):
        return pl.ds(half * 256 + quarter * 128, 128)

    scatter = {}

    def lanes_of(wave):
        return pl.ds(wave * 128, 128)

    def term(wave, half, first, by, quarter):
        along, across = (by, slice(None)) if first else (0, by)
        place = (along, across) if half == 0 else (across, along)
        return wt.at[place[0], place[1], wrows(half, quarter), lanes_of(wave)]

    def landing(wave, half, first, kind):
        return (rfirst if first else rlast).at[wave, half, kind]

    def scatter_make(wave, half, first, kind, by, quarter, to):
        scatter[wave, half, first, kind] = remote(
            term(wave, half, first, by, quarter),
            landing(wave, half, first, kind),
            peer(*step(half, first, to)),
        )
        return scatter[wave, half, first, kind]

    def scatter_open(wave, first):
        copies = []
        for kind, by, quarter, to in ((0, 2, 0, 1), (1, 2, 1, 3), (2, 1, 1, 1), (3, 3, 0, 3)):
            for half in (0, 1):
                copies.append(scatter_make(wave, half, first, kind, by, quarter, to))
        return copies

    def add_in(wave, half, first, by, quarter, kinds):
        total = term(wave, half, first, by, quarter)[...].astype(F32)
        for kind in kinds:
            total = total + landing(wave, half, first, kind)[...].astype(F32)
        return total

    def scatter_forward(wave, first):
        for half in (0, 1):
            for kind, by, quarter in ((0, 1, 0), (1, 3, 1)):
                scatter[wave, half, first, kind].wait_recv()
                total = add_in(wave, half, first, by, quarter, (kind,))
                term(wave, half, first, by, quarter)[...] = total.astype(BF16)
                scatter_make(wave, half, first, kind + 4, by, quarter, by).start()

    def scatter_own(wave, first):
        for half in (0, 1):
            for kind in (2, 3, 4, 5):
                scatter[wave, half, first, kind].wait_recv()
            for quarter, kinds in ((0, (3, 4)), (1, (2, 5))):
                total = add_in(wave, half, first, 0, quarter, kinds)
                if first:
                    term(wave, half, first, 0, quarter)[...] = total.astype(BF16)
                else:
                    fin[wave, half * 2 + quarter] = total

    after, before, across = lax.rem(rep + 1, 4), lax.rem(rep + 3, 4), lax.rem(rep + 2, 4)
    halves = (slice(0, 64), slice(64, 128))
    rep_copies = {}

    def rep_send(wave, kind, value, to):
        rep_stage[wave, kind] = value.astype(BF16)
        rep_copies[wave, kind] = send(rep_stage.at[wave, kind], rep_recv.at[wave, kind], {"rep": to})

    def rep_got(wave, kind):
        rep_copies[wave, kind].wait_recv()
        return rep_recv[wave, kind].astype(F32)

    def rep_stage_of(wave, stage):
        if stage == 0:
            rep_send(wave, 0, fin[wave, across, halves[0], :], after)
            rep_send(wave, 1, fin[wave, across, halves[1], :], before)
            rep_send(wave, 2, fin[wave, after, halves[1], :], after)
            rep_send(wave, 3, fin[wave, before, halves[0], :], before)
        elif stage == 1:
            rep_send(wave, 4, fin[wave, after, halves[0], :] + rep_got(wave, 0), after)
            rep_send(wave, 5, fin[wave, before, halves[1], :] + rep_got(wave, 1), before)
        elif stage == 2:
            for half, kinds in ((0, (3, 4)), (1, (2, 5))):
                total = fin[wave, rep, halves[half], :]
                for kind in kinds:
                    total = total + rep_got(wave, kind)
                rep_all[wave, rep, halves[half], :] = total.astype(BF16)
            for kind, to in ((6, after), (7, before)):
                here = rep_all.at[wave, rep]
                rep_copies[wave, kind] = send(here, here, {"rep": to})
        elif stage == 3:
            for kind, part, half, to in ((6, before, 0, after), (7, after, 1, before)):
                rep_copies[wave, kind].wait_recv()
                here = rep_all.at[wave, part, pl.ds(64 * half, 64), :]
                rep_copies[wave, kind + 2] = send(here, here, {"rep": to})
        else:
            for kind in (8, 9):
                rep_copies[wave, kind].wait_recv()

    def scatter_stage(wave, stage):
        if stage == 0:
            scatter_forward(wave, True)
        elif stage == 1:
            scatter_own(wave, True)
            for copy in scatter_open(wave, False):
                copy.start()
        elif stage == 2:
            scatter_forward(wave, False)
        elif stage == 3:
            scatter_own(wave, False)
            rep_stage_of(wave, 0)

    opening = scatter_open(0, True) + scatter_open(1, True)

    def open_scatter():
        for copy in opening:
            copy.start()

    for place in range(0, 7):
        value_block(place)
    for half in (0, 1):
        gather_forward(half, False, 3, 2)
    pl.when(is_low)(open_scatter)
    for place in range(7, 11):
        value_block(place)
    for half in (0, 1):
        gather_end(half, False, 1)
        gather_end(half, False, 2)
    for place in range(11, 15):
        value_block(place)
    for half in (0, 1):
        gather_end(half, False, 3)
    pl.when(is_top)(open_scatter)
    value_block(15)
    send_part = send(vpart.at[pl.ds(TOK, TOK), :], vrecv, sibling)
    for place in range(EARLY, EARLY + 4):
        grad_block(place)

    send_part.wait_recv()
    whole = vpart[0:TOK, :] + vrecv[...]
    values[...] = whole.astype(BF16)
    mean = jnp.sum(whole * vg[0:TOK, :].astype(F32), axis=1, keepdims=True) * (1.0 / D)
    cen[...] = jnp.broadcast_to(mean, (TOK, 128))
    cen_row[...] = cen[...].T[0:8, :]
    send_cen1 = remote(cen_row, cen1_row, below, "down")

    load_top.wait()

    def branch(hidden, scale, grad, gain_row, center):
        factor = scale[:, 0:1]
        normalized = hidden.astype(F32) * factor
        return factor * (grad.astype(F32) * gain_row - normalized * center[:, 0:1])

    def own_branch(where):
        return branch(hid[:, where], inv, ng[:, where], gain[:, where], cen)

    lates = []
    for e in range(EARLY, 16):
        j = chip_at(*ORDER[e])
        where = cols(j * 512, 512)
        lates.append((j, remote(
            stream.at[:, where], late.at[:, pl.ds((e - EARLY) * 512, 512)], below, "down"
        )))
    def top_block(j):
        where = cols(j * 512, 512)
        stream[:, where] = (top[:, where].astype(F32) + own_branch(where)).astype(BF16)

    def own_blocks(start, stop):
        @pl.when(is_low)
        def _():
            for place in range(start, stop):
                where = cols(chip_at(*ORDER[place]) * 512, 512)
                own[:, where] = own_branch(where)

    def send_lates(start, stop):
        grads_ready(EARLY + start, EARLY + stop)
        own_blocks(EARLY + start, EARLY + stop)

        @pl.when(is_top)
        def _():
            if start == 0:
                send_cen1.start()
            for j, copy in lates[start:stop]:
                top_block(j)
                copy.start()

    def top_early(start, stop):
        grads_ready(start, stop)
        own_blocks(start, stop)

        @pl.when(is_top)
        def _():
            for j, _, _ in early[start:stop]:
                top_block(j)

    send_lates(0, 2)
    scatter_stage(0, 0)
    for place in range(EARLY + 4, 16):
        grad_block(place)
    send_lates(2, 4)
    scatter_stage(1, 0)
    send_lates(4, 6)
    scatter_stage(0, 1)
    send_lates(6, 16 - EARLY)
    for place in range(0, EARLY):
        grad_block(place)

    def attend_back(k):
        lanes = slice(k * HEAD, (k + 1) * HEAD)
        queries, grads = stacked(query, k), stacked(ctx, k)
        prob = probs[k]
        grad_prob = dot_nt(values[:, lanes], grads)
        row_dot = jnp.sum(prob * grad_prob, axis=0, keepdims=True)
        wide = prob * (grad_prob - row_dot) * SCORE_SCALE
        grad_score = wide.astype(BF16)
        kg[:, lanes] = dot(grad_score, queries).astype(BF16)
        for g in range(GROUP):
            turned = wide[:, g * HEAD:(g + 1) * HEAD].T.astype(BF16)
            head = (GROUP * k + g) * HEAD
            qg[:, head:head + HEAD] = dot(turned, key[:, lanes]).astype(BF16)

    ng1_copies = []
    forward_vg1 = remote(vg1.at[pl.ds(0, TOK), :], vg1.at[pl.ds(TOK, TOK), :], sibling, "low")
    for e in range(EARLY):
        where = cols(e * 512 + core * BLK, BLK)
        ng1_copies.append(remote(ng1_stage.at[e], ng1.at[:, where], sibling, "low"))

    @pl.when(is_low)
    def _():
        send_vg1.wait_recv()
        forward_vg1.start()

    def early_grads(start, stop):
        @pl.when(is_low)
        def _():
            if start == 0:
                forward_vg1.wait_recv()
            for e in range(start, stop):
                for half in (0, 1):
                    early[e][2][half].wait_recv()
                grad = dot_nt(vg1[...], w1[e])
                ng1[:, cols(e * 512 + core * BLK, BLK)] = grad[0:TOK].astype(BF16)
                ng1_stage[e] = grad[TOK:].astype(BF16)
                ng1_copies[e].start()

    wown[...] = w_all[chip].astype(F32).T

    def finish(wave):
        rep_stage_of(wave, 4)
        summed = jnp.concatenate([rep_all[wave, q].astype(F32) for q in range(4)], axis=0) * GRAD_SCALE
        here = slice(wave * 128, wave * 128 + 128)
        vwg[here, :] = summed.T
        gain_own = gain[:, cols(shard * BLK + wave * 128, 128)]
        gg[:, here] = jnp.sum(summed * wown[:, here], axis=0, keepdims=True) / gain_own

    scatter_stage(0, 2)
    attend_back(0)
    scatter_stage(1, 1)
    scatter_stage(0, 3)
    scatter_stage(1, 2)
    attend_back(1)
    rep_stage_of(0, 1)
    scatter_stage(1, 3)
    attend_back(2)
    rep_stage_of(0, 2)
    rep_stage_of(1, 1)
    attend_back(3)
    early_grads(0, 2)
    rep_stage_of(0, 3)
    rep_stage_of(1, 2)
    early_grads(2, EARLY)
    top_early(0, 4)
    rep_stage_of(1, 3)
    top_early(4, EARLY)
    finish(0)

    @pl.when(is_low)
    def _():
        send_inv1.wait_recv()
        send_gain1.wait_recv()
        send_cen1.wait_recv()
        inv1[...] = jnp.broadcast_to(inv1_row[0:1, :], (TOK, 128)).T
        cen1[...] = jnp.broadcast_to(cen1_row[0:1, :], (TOK, 128)).T
        for e in range(EARLY):
            ng1_copies[e].wait_recv()
            early[e][1].wait_recv()
            here = pl.ds(e * 512, 512)
            where = cols(early[e][0] * 512, 512)
            upper = branch(hid1[:, here], inv1, ng1[:, here], gain1[:, where], cen1)
            upper = (top[:, where].astype(F32) + upper).astype(BF16)
            stream[:, where] = (upper.astype(F32) + own[:, where]).astype(BF16)
        for e, (j, copy) in enumerate(lates):
            copy.wait_recv()
            where = cols(j * 512, 512)
            upper = late[:, pl.ds(e * 512, 512)].astype(F32)
            stream[:, where] = (upper + own[:, where]).astype(BF16)

    finish(1)

    for copy, who in sent:
        if who is None:
            copy.wait_send()

    @pl.when(is_top)
    def _():
        for copy, who in sent:
            if who == "down":
                copy.wait_send()

    @pl.when(is_low)
    def _():
        for copy, who in sent:
            if who == "low":
                copy.wait_send()


def store_kernel(*refs):
    parts, outs, sems = refs[:5], refs[5:10], refs[10]
    copies = [pltpu.make_async_copy(parts[n], outs[n], sems.at[n]) for n in range(5)]
    for copy in copies:
        copy.start()
    for copy in copies:
        copy.wait()


def per_device(hidden_in, query_rows, key_rows, context_grad, stream_top, norm_gain, value_weight):
    def vmem(*shape, dtype=BF16):
        return pltpu.VMEM(shape, dtype)

    scratch = [
        vmem(TOK, D), vmem(TOK, D // 2), vmem(TOK, 4096), vmem(TOK, KVW), vmem(TOK, 4096), vmem(TOK, D),
        vmem(1, D, dtype=F32), vmem(1, D, dtype=F32),
        *[vmem(TOK, 128, dtype=F32) for _ in range(5)], *[vmem(8, 128, dtype=F32) for _ in range(4)],
        vmem(16, BLK, KVW), vmem(EARLY, BLK, KVW), vmem(2 * TOK, 4096),
        vmem(2 * TOK, KVW), vmem(2 * TOK, KVW), vmem(KVW, 2 * TOK),
        vmem(KV, TOK, GROUP * TOK, dtype=F32),
        vmem(2 * TOK, KVW, dtype=F32), vmem(TOK, KVW, dtype=F32), vmem(TOK, KVW),
        vmem(TOK, D), vmem(16, TOK, BLK), vmem(TOK, EARLY * 512), vmem(EARLY, TOK, BLK),
        vmem(TOK, EARLY * 512), vmem(TOK, (16 - EARLY) * 512), vmem(TOK, D, dtype=F32),
        vmem(4, 4, KVW, BLK), vmem(2, 2, 6, 4, 128, 128), vmem(2, 2, 6, 128, 128), vmem(2, 4, 128, 128, dtype=F32),
        vmem(2, 6, 64, 128), vmem(2, 6, 64, 128), vmem(2, 4, 128, 128), vmem(KVW, BLK, dtype=F32),
        pltpu.SemaphoreType.DMA((NSEM,)), pltpu.SemaphoreType.DMA((NSEM,)), pltpu.SemaphoreType.DMA((32,)),
    ]
    out_shapes = (((TOK, D), BF16), ((TOK, 4096), BF16), ((TOK, KVW), BF16), ((BLK, KVW), F32), ((1, BLK), F32))
    args = hidden_in[0], query_rows[0], key_rows[0], context_grad[0], stream_top, norm_gain, value_weight[0]
    parts = pl.pallas_call(
        kernel,
        out_shape=tuple(pltpu.VMEM(*shape) for shape in out_shapes),
        in_specs=[pl.BlockSpec(memory_space=pl.ANY)] * 7,
        out_specs=[pl.BlockSpec(memory_space=pltpu.VMEM)] * 5,
        scratch_shapes=scratch,
        compiler_params=pltpu.CompilerParams(
            collective_id=0, has_side_effects=True, vmem_limit_bytes=48 * 1024 * 1024
        ),
        cost_estimate=pl.CostEstimate(flops=5 * 10**9, bytes_accessed=12 * 10**6, transcendentals=10**6),
    )(*[pltpu.with_memory_space_constraint(arg, pltpu.HBM) for arg in args])
    outs = pl.pallas_call(
        store_kernel,
        out_shape=tuple(jax.ShapeDtypeStruct(*shape) for shape in out_shapes),
        in_specs=[pl.BlockSpec(memory_space=pltpu.VMEM)] * 5,
        out_specs=[pl.BlockSpec(memory_space=pl.ANY)] * 5,
        scratch_shapes=[pltpu.SemaphoreType.DMA((5,))],
        compiler_params=pltpu.CompilerParams(vmem_limit_bytes=1024 * 1024),
    )(*[pltpu.with_memory_space_constraint(part, pltpu.VMEM) for part in parts])
    stream, query_grad, key_grad, weight_grad, gain_grad = outs
    return stream[None], query_grad[None], key_grad[None], weight_grad[None], gain_grad


def solution(mesh):
    return jax.shard_map(
        per_device,
        mesh=mesh,
        in_specs=(
            P("pipe", ("rep", "shard"), None),
            P("pipe", ("rep", "shard"), None),
            P("pipe", ("rep", "shard"), None),
            P("pipe", ("rep", "shard"), None),
            P(("rep", "shard"), None),
            P("pipe", None),
            P("pipe", "shard", None),
        ),
        out_specs=(
            P("pipe", ("rep", "shard"), None),
            P("pipe", ("rep", "shard"), None),
            P("pipe", ("rep", "shard"), None),
            P("pipe", "shard", None),
            P("pipe", "shard"),
        ),
        check_vma=False,
    )
```
